32 devices in a mesh: section: 2 (over x), seq: 4 (over z), mp: 4 (over y, core).
Axes of the slice: x: 2, y: 2, z: 4, core: 2. Of those that a mesh axis runs over, the one named last changes fastest.
Arguments:
- video: bfloat16 [2, 4, 32, 3072], P(None, None, 'seq'), may hold values from -6 to 6
- text: bfloat16 [2, 32, 3072], P(None, 'seq'), may hold values from -6 to 6
- patch_lengths: int32 [2, 4], replicated, may hold values from 1 to 32, 96 in all within a row
- text_len: int32 [2], replicated, may hold values from 16 to 32, as said below
- timestep: int32 [1], replicated, may hold values from 0 to 999
- w_mod: bfloat16 [2, 512, 9216], P('section', None, 'mp'), may hold values from -0.25 to 0.25
- w_qkv: bfloat16 [2, 3072, 3, 3072], P('section', None, None, 'mp')
- w_out: bfloat16 [2, 3072, 3072], P('section', 'mp'), may hold values from -0.109375 to 0.109375
- stale_cache: bfloat16 [2, 2, 4, 32, 2, 3072], P('section', None, None, 'seq', None, 'mp'), may hold values from -6 to 6
Outputs:
- hidden_video: bfloat16 [2, 2, 4, 32, 3072], P('section', None, None, 'seq')
- hidden_text: bfloat16 [2, 2, 32, 3072], P('section', None, 'seq')
- cache_video: bfloat16 [2, 2, 4, 32, 2, 3072], P('section', None, None, 'seq', None, 'mp')
- cache_text: bfloat16 [2, 2, 32, 2, 3072], P('section', None, 'seq', None, 'mp')
The draws below stay inside these ranges and needn't reach their ends.
Inputs may be any that keep to these rules, and one draw needn't show every extreme that they name: `patch_lengths`: 4 patch lengths per request summing to 96; in every request the largest is 32. `text_len`: exactly one request has 32, every other fewer.
All inputs are finite; a program needn't handle non-finite values.
Results may differ from the reference program's by a relative error of at most 0.01.
Values may be sent and summed in bfloat16 or wider, within the bound.
A program may use at most 192 MiB of HBM per device.

```python
import math
import jax
import jax.numpy as jnp
import numpy as np
from jax import lax

D = 3072
HEAD = 64
TE = 512
REQS = 2
NPATCH = 4
HD = 3072
PCAP = 32
VIDEO = 96
TEXT = 32


def draw_text_len(key, part):
    lengths = jax.random.randint(key, (REQS,), TEXT // 2, TEXT)
    chosen = jax.random.randint(jax.random.fold_in(key, 3), (), 0, REQS)
    return jnp.where(jnp.arange(REQS) == chosen, TEXT, lengths).astype(jnp.int32)


def draw_w_qkv(key, part):
    drawn = jax.random.normal(key, (2, D, 3, HD), jnp.float32) * D ** (-0.5)
    return drawn.astype(jnp.bfloat16)


def block_scale(rng, shape, shards, smallest, high):
    factor_of = 1.0
    for axis_at, blocks in shards:
        steps = jax.random.uniform(jax.random.fold_in(jax.random.fold_in(rng, 6), axis_at), (blocks,), jnp.float32, smallest / len(shards), high / len(shards))
        factor_of = factor_of * jnp.repeat(jnp.exp(steps), shape[axis_at] // blocks).reshape((-1,) + (1,) * (len(shape) - 1 - axis_at))
    return factor_of


def split_up(amount, total, reach, lean):
    portions = [(1 << 20) // math.isqrt(standing ** lean) + 1 for standing in range(2, amount + 1)]
    rest, holding = total - reach - (amount - 1), [1] * (amount - 1)
    while rest > 0:
        movable = [i for i in range(amount - 1) if holding[i] < reach]
        whole, remaining = sum([portions[i] for i in movable]), rest
        for i in movable:
            extra = min(reach - holding[i], max(1, remaining * portions[i] // whole), rest)
            holding[i] = holding[i] + extra
            rest = rest - extra
    return np.array([reach] + holding)


def uneven_parts(key, amount, total, limit, skew):
    if amount == 2:
        one = jax.random.randint(key, (), max(1, total - limit), min(limit, total - 1) + 1)
        return jnp.stack([one, total - one])
    sizes = jnp.asarray(split_up(amount, total, limit, skew), jnp.int32)
    twos = (amount - 1) // 2
    donor, taker = sizes[1:1 + 2 * twos:2], sizes[2:2 + 2 * twos:2]
    margin = jnp.minimum(donor - 1, limit - taker)
    shifted = jax.random.randint(jax.random.fold_in(key, 1), (twos,), 0, 1 << 20) % (margin + 1)
    sizes = sizes.at[1:1 + 2 * twos:2].set(donor - shifted).at[2:2 + 2 * twos:2].set(taker + shifted)
    return sizes[jax.random.permutation(jax.random.fold_in(key, 2), amount)]


def scatter_about(stream_key, extent, deviation, most, split=(), held_as=jnp.bfloat16):
    values = deviation * jax.random.normal(stream_key, extent, jnp.float32)
    if split:
        values = values * block_scale(stream_key, extent, split, -0.22, 0.18)
    return jnp.clip(values, -most, most).astype(held_as)


def setup_inputs(seed: int = 0) -> dict:
    arg_keys = jax.random.split(jax.random.key(seed), 10)
    video = scatter_about(arg_keys[0], (REQS, NPATCH, PCAP, D), 1.0, 6.0, ((2, 4),))
    text = scatter_about(arg_keys[1], (REQS, TEXT, D), 1.0, 6.0, ((1, 4),))
    patch_lengths = jax.vmap(lambda own: uneven_parts(own, NPATCH, VIDEO, PCAP, 2))(jax.random.split(arg_keys[2], REQS)).reshape((REQS, NPATCH)).astype(jnp.int32)
    text_len = draw_text_len(jax.random.fold_in(arg_keys[9], 71), 0)
    timestep = jax.random.randint(arg_keys[4], (1,), 0, 1000).astype(jnp.int32)
    w_mod = scatter_about(arg_keys[5], (2, TE, 3 * D), TE ** -0.5, 0.25, ((0, 2), (2, 4)))
    w_qkv = draw_w_qkv(jax.random.fold_in(arg_keys[9], 71), 0)
    w_out = scatter_about(arg_keys[7], (2, HD, D), HD ** -0.5, 0.109375, ((0, 2), (1, 4)))
    stale_cache = scatter_about(arg_keys[8], (2, REQS, NPATCH, PCAP, 2, HD), 1.0, 6.0, ((0, 2), (3, 4), (5, 4)))
    return {"video": video, "text": text, "patch_lengths": patch_lengths, "text_len": text_len, "timestep": timestep, "w_mod": w_mod, "w_qkv": w_qkv, "w_out": w_out, "stale_cache": stale_cache}


EPS = 1e-05
NEG = -1e+30

def modulation(timestep, weight):
    half_width = weight.shape[0] // 2
    frequency = jnp.exp(-math.log(10000.0) * jnp.arange(half_width, dtype=jnp.float32) / half_width)
    phases = timestep.astype(jnp.float32)[0] * frequency
    embedding = jnp.concatenate([jnp.cos(phases), jnp.sin(phases)])
    active = jax.nn.silu(embedding).astype(jnp.bfloat16)
    return jnp.dot(active[None, :], weight, preferred_element_type=jnp.float32)[0]

def normalize(token_rows, shift_vec, scale_vec):
    values = token_rows.astype(jnp.float32)
    center = values - lax.optimization_barrier(jnp.mean(values, axis=-1, keepdims=True))
    spread = lax.optimization_barrier(jnp.mean(center * center, axis=-1, keepdims=True))
    return (center * lax.rsqrt(spread + EPS) * (1.0 + scale_vec) + shift_vec).astype(jnp.bfloat16)

def masked_terms(queries, key_heads, value_heads, key_mask):
    scores = jnp.einsum('rqe,rke->rqk', queries.astype(jnp.float32), key_heads.astype(jnp.float32)) * HEAD ** (-0.5)
    top_score = lax.optimization_barrier(jnp.max(jnp.where(key_mask, scores, NEG), axis=-1))
    weights = jnp.where(key_mask, jnp.exp(scores - top_score[..., None]), 0.0)
    weight_sum = lax.optimization_barrier(jnp.sum(weights, axis=-1))
    accumulated = jnp.einsum('rqk,rke->rqe', weights.astype(jnp.bfloat16).astype(jnp.float32), value_heads.astype(jnp.float32))
    return (top_score, weight_sum, accumulated)

def apply_layer(video, text, weight_mod, weight_qkv, weight_out, stale, patch_lengths, text_len, timestep):
    requests, patches, capacity, model_width = video.shape
    text_slots = text.shape[1]
    modulated = modulation(timestep, weight_mod)
    shift_vec = modulated[:model_width]
    scale_vec = modulated[model_width:2 * model_width]
    gate_vec = modulated[2 * model_width:]
    token_rows = jnp.concatenate([video.reshape(requests, patches * capacity, model_width), text], axis=1)
    row_count = token_rows.shape[1]
    normed = normalize(token_rows, shift_vec, scale_vec)
    column_count = weight_out.shape[0]
    head_count = column_count // HEAD
    projected = jnp.dot(normed.reshape(-1, model_width), weight_qkv.reshape(model_width, 3 * column_count), preferred_element_type=jnp.float32)
    projected = projected.reshape(requests, row_count, 3, column_count).astype(jnp.bfloat16)

    def split_heads(array):
        return array.reshape(requests, array.shape[1], head_count, HEAD).transpose(2, 0, 1, 3)
    video_patch = jnp.repeat(jnp.arange(patches, dtype=jnp.int32), capacity)
    all_patch = jnp.concatenate([video_patch, jnp.zeros((text_slots,), jnp.int32)])
    slot_index = jnp.arange(capacity, dtype=jnp.int32)
    video_valid = (slot_index[None, None, :] < patch_lengths[:, :, None]).reshape(requests, -1)
    text_valid = jnp.arange(text_slots, dtype=jnp.int32)[None, :] < text_len[:, None]
    all_valid = jnp.concatenate([video_valid, text_valid], axis=1)
    fresh_mask = all_valid[:, None, :] & (all_patch[None, None, :] <= all_patch[None, :, None])
    stale_mask = video_valid[:, None, :] & (video_patch[None, None, :] > all_patch[None, :, None])
    stale_flat = stale.reshape(requests, patches * capacity, 2, column_count)

    def per_head(pieces):
        query_h, key_h, value_h, stale_key_h, stale_value_h = pieces
        fresh_top, fresh_sum, fresh_acc = masked_terms(query_h, key_h, value_h, fresh_mask)
        stale_top, stale_sum, stale_acc = masked_terms(query_h, stale_key_h, stale_value_h, stale_mask)
        top_score = jnp.maximum(fresh_top, stale_top)
        fresh_weight = jnp.exp(fresh_top - top_score)
        stale_weight = jnp.exp(stale_top - top_score)
        numer = fresh_acc * fresh_weight[..., None] + stale_acc * stale_weight[..., None]
        denom = fresh_sum * fresh_weight + stale_sum * stale_weight
        return (numer / denom[..., None]).astype(jnp.bfloat16)
    outputs = lax.map(per_head, (split_heads(projected[:, :, 0]), split_heads(projected[:, :, 1]), split_heads(projected[:, :, 2]), split_heads(stale_flat[:, :, 0]), split_heads(stale_flat[:, :, 1])))
    attended = outputs.transpose(1, 2, 0, 3).reshape(requests, row_count, column_count)
    mixed_rows = jnp.dot(attended.reshape(-1, column_count), weight_out, preferred_element_type=jnp.float32).reshape(requests, row_count, model_width)
    result = (token_rows.astype(jnp.float32) + gate_vec * mixed_rows).astype(jnp.bfloat16)
    key_value = projected[:, :, 1:]
    split_at = patches * capacity
    return (result[:, :split_at].reshape(video.shape), result[:, split_at:], key_value[:, :split_at].reshape(requests, patches, capacity, 2, column_count), key_value[:, split_at:])

def reference(video, text, patch_lengths, text_len, timestep, w_mod, w_qkv, w_out, stale_cache):
    layer_one = apply_layer(video, text, w_mod[0], w_qkv[0], w_out[0], stale_cache[0], patch_lengths, text_len, timestep)
    layer_two = apply_layer(layer_one[0], layer_one[1], w_mod[1], w_qkv[1], w_out[1], stale_cache[1], patch_lengths, text_len, timestep)
    return (jnp.stack([layer_one[0], layer_two[0]]), jnp.stack([layer_one[1], layer_two[1]]), jnp.stack([layer_one[2], layer_two[2]]), jnp.stack([layer_one[3], layer_two[3]]))
```

```python
import functools
import math

import jax
import jax.numpy as jnp
from jax import lax
from jax.experimental import pallas as pl
from jax.experimental.pallas import tpu as pltpu
from jax.sharding import PartitionSpec as P

HEAD = 64
EPS = 1e-05
NEG = -1e30
SLAB = 128
GROUP = 256
MESH = pl.DeviceIdType.MESH
F32 = jnp.float32
BF16 = jnp.bfloat16


def slot_marks(index, lengths_ref, text_ref, requests, first, patches, per_dev, text_dev, owner):
    req = jnp.zeros_like(index)
    patch = jnp.zeros_like(index)
    limit = jnp.zeros_like(index)
    start = jnp.zeros_like(index)
    at = 0
    for r in range(requests):
        for p in range(first, patches):
            inside = (index >= at) & (index < at + per_dev)
            req = jnp.where(inside, r, req)
            patch = jnp.where(inside, p, patch)
            limit = jnp.where(inside, lengths_ref[r, p], limit)
            start = jnp.where(inside, at, start)
            at += per_dev
    width = jnp.full_like(index, per_dev)
    for r in range(requests if text_dev else 0):
        inside = (index >= at) & (index < at + text_dev)
        req = jnp.where(inside, r, req)
        limit = jnp.where(inside, text_ref[r], limit)
        start = jnp.where(inside, at, start)
        width = jnp.where(inside, text_dev, width)
        at += text_dev
    live = owner * width + index - start < limit
    return req, patch, live


def split_index(shape, dim, size, count):
    index = lax.broadcasted_iota(jnp.int32, shape, dim)
    owner = jnp.zeros_like(index)
    for j in range(1, count):
        owner = owner + jnp.where(index >= j * size, 1, 0)
    return owner, index - owner * size


def kernel(dims, lengths_ref, text_len_ref, act_ref, video_ref, text_ref, stale_ref, w_mod_hbm,
           w_qkv_hbm, w_out_hbm, hidden_video, hidden_text, cache_video, cache_text,
           w_mod, w_qkv, w_out, x_buf, normed, query, attended, result, mod_all, kv_all, stale_all,
           part_send, part_recv, bias_f, bias_s,
           w_sem, mod_send, mod_recv, stale_send, stale_recv, kv_send, kv_recv, p_send, p_recv,
           x_cross_send, x_fwd_send, x_recv, res_send, res_recv):
    requests, patches, per_dev, text_dev, n_seq, n_mp, width, cols = dims
    rows = requests * (patches * per_dev + text_dev)
    video_rows = requests * patches * per_dev
    stale_rows = stale_ref.shape[1]
    groups = cols // GROUP
    section = lax.axis_index("section")
    seq = lax.axis_index("seq")
    mp = lax.axis_index("mp")
    other = 1 - section

    def at(sec, se, m):
        return (sec, se, m)

    weight_copies = [pltpu.make_async_copy(w_mod_hbm, w_mod, w_sem.at[0])]
    pieces = 3
    piece = width // pieces
    for part in (1, 2, 0):
        for i in range(pieces):
            weight_copies.append(pltpu.make_async_copy(
                w_qkv_hbm.at[part, pl.ds(i * piece, piece)],
                w_qkv.at[part, pl.ds(i * piece, piece)],
                w_sem.at[1 + part * pieces + i]))
    weight_copies.append(pltpu.make_async_copy(w_out_hbm, w_out, w_sem.at[1 + 3 * pieces]))
    for copy in weight_copies:
        copy.start()

    barrier = pltpu.get_barrier_semaphore()
    for k in range(1, n_mp):
        pl.semaphore_signal(barrier, inc=1, device_id=at(section, seq, lax.rem(mp + k, n_mp)), device_id_type=MESH)
    for k in range(1, n_seq):
        pl.semaphore_signal(barrier, inc=1, device_id=at(section, lax.rem(seq + k, n_seq), mp), device_id_type=MESH)
    pl.semaphore_signal(barrier, inc=1, device_id=at(other, seq, mp), device_id_type=MESH)

    weight_copies[0].wait()
    mod_all[mp] = jnp.dot(act_ref[...], w_mod[...], preferred_element_type=F32)
    stale_all[seq] = stale_ref[...]
    pl.semaphore_wait(barrier, n_mp - 1 + n_seq - 1 + 1)

    def mod_copy(k):
        return pltpu.make_async_remote_copy(
            src_ref=mod_all.at[mp], dst_ref=mod_all.at[mp], send_sem=mod_send.at[k],
            recv_sem=mod_recv.at[k], device_id=at(section, seq, lax.rem(mp + k, n_mp)), device_id_type=MESH)

    def mod_arrival(k):
        origin = lax.rem(mp + n_mp - k, n_mp)
        return pltpu.make_async_remote_copy(
            src_ref=mod_all.at[origin], dst_ref=mod_all.at[origin], send_sem=mod_send.at[k],
            recv_sem=mod_recv.at[k], device_id=at(section, seq, origin), device_id_type=MESH)

    def stale_copy(k, origin):
        return pltpu.make_async_remote_copy(
            src_ref=stale_all.at[origin], dst_ref=stale_all.at[origin], send_sem=stale_send.at[k],
            recv_sem=stale_recv.at[k], device_id=at(section, lax.rem(seq + k, n_seq), mp), device_id_type=MESH)

    for k in range(1, n_mp):
        mod_copy(k).start()
    for k in range(1, n_seq):
        stale_copy(k, seq).start()

    row_head, row_index = split_index((2 * rows, 1), 0, rows, 2)
    row_req, row_patch, _ = slot_marks(
        row_index, lengths_ref, text_len_ref, requests, 0, patches, per_dev, text_dev, row_head)
    key_owner, key_index = split_index((1, n_seq * rows), 1, rows, n_seq)
    key_req, key_patch, key_live = slot_marks(
        key_index, lengths_ref, text_len_ref, requests, 0, patches, per_dev, text_dev, key_owner)
    key_limit = jnp.where(key_live, key_patch, patches)
    bias_f[...] = jnp.where((row_req == key_req) & (key_limit <= row_patch), 0.0, NEG)
    key_owner, key_index = split_index((1, n_seq * stale_rows), 1, stale_rows, n_seq)
    key_req, key_patch, key_live = slot_marks(
        key_index, lengths_ref, text_len_ref, requests, 1, patches, per_dev, 0, key_owner)
    key_limit = jnp.where(key_live, key_patch, -1)
    bias_s[...] = jnp.where((row_req == key_req) & (key_limit > row_patch), 0.0, NEG)

    @pl.when(section == 0)
    def _():
        x_buf[pl.ds(0, video_rows)] = video_ref[...]
        x_buf[pl.ds(video_rows, rows - video_rows)] = text_ref[...]

    def block(j):
        return pl.ds(pl.multiple_of(j * cols, SLAB), cols)

    def cross_copy():
        return pltpu.make_async_remote_copy(
            src_ref=result.at[:, block(mp)], dst_ref=x_buf.at[:, block(mp)], send_sem=x_cross_send,
            recv_sem=x_recv.at[0], device_id=at(other, seq, mp), device_id_type=MESH)

    def forward_copy(k, origin):
        return pltpu.make_async_remote_copy(
            src_ref=x_buf.at[:, block(origin)], dst_ref=x_buf.at[:, block(origin)], send_sem=x_fwd_send.at[k],
            recv_sem=x_recv.at[k], device_id=at(section, seq, lax.rem(mp + k, n_mp)), device_id_type=MESH)

    for k in range(1, n_mp):
        mod_arrival(k).wait_recv()

    @pl.when(section == 1)
    def _():
        cross_copy().wait_recv()
        for k in range(1, n_mp):
            forward_copy(k, mp).start()
        for k in range(1, n_mp):
            forward_copy(k, lax.rem(mp + n_mp - k, n_mp)).wait_recv()

    def modulated(b):
        return mod_all[b // 3, 0:1, (b % 3) * cols:(b % 3 + 1) * cols]

    values = x_buf[...].astype(F32)
    mean = jnp.mean(values, axis=-1, keepdims=True)
    center = values - mean
    inverse = lax.rsqrt(jnp.mean(center * center, axis=-1, keepdims=True) + EPS)
    for c in range(n_mp):
        span = slice(c * cols, (c + 1) * cols)
        piece_values = (x_buf[:, span].astype(F32) - mean) * inverse
        normed[:, span] = (piece_values * (1.0 + modulated(n_mp + c)) + modulated(c)).astype(BF16)

    def kv_copy(g, k, origin):
        return pltpu.make_async_remote_copy(
            src_ref=kv_all.at[g, origin], dst_ref=kv_all.at[g, origin], send_sem=kv_send.at[g, k],
            recv_sem=kv_recv.at[g, k], device_id=at(section, lax.rem(seq + k, n_seq), mp), device_id_type=MESH)

    def project(part, g):
        return jnp.dot(normed[...], w_qkv[part, :, g * GROUP:(g + 1) * GROUP], preferred_element_type=F32)

    for copy in weight_copies[1:1 + pieces]:
        copy.wait()
    for g in range(groups):
        span = slice(g * GROUP, (g + 1) * GROUP)
        key = project(1, g).astype(BF16)
        if g == 0:
            for copy in weight_copies[1 + pieces:1 + 2 * pieces]:
                copy.wait()
        value = project(2, g).astype(BF16)
        kv_all[g, seq, :, 0:GROUP] = key
        kv_all[g, seq, :, GROUP:2 * GROUP] = value
        for k in range(1, n_seq):
            kv_copy(g, k, seq).start()
        cache_video[:, span] = key[:video_rows]
        cache_text[:, span] = key[video_rows:]
        span = slice(cols + g * GROUP, cols + (g + 1) * GROUP)
        cache_video[:, span] = value[:video_rows]
        cache_text[:, span] = value[video_rows:]
    for copy in weight_copies[1 + 2 * pieces:1 + 3 * pieces]:
        copy.wait()
    for g in range(groups):
        query[:, g * GROUP:(g + 1) * GROUP] = (project(0, g).astype(BF16).astype(F32) * HEAD ** (-0.5)).astype(BF16)

    for k in range(1, n_seq):
        stale_copy(k, lax.rem(seq + n_seq - k, n_seq)).wait_recv()
    low = lax.broadcasted_iota(jnp.int32, (rows, SLAB), 1) < HEAD
    contract_last = (((1,), (1,)), ((), ()))
    for g in range(groups):
        for k in range(1, n_seq):
            kv_copy(g, k, lax.rem(seq + n_seq - k, n_seq)).wait_recv()
        for h in range(GROUP // SLAB):
            span = slice(g * GROUP + h * SLAB, g * GROUP + (h + 1) * SLAB)
            k_span = slice(h * SLAB, (h + 1) * SLAB)
            v_span = slice(GROUP + h * SLAB, GROUP + (h + 1) * SLAB)
            slab = query[:, span]
            zero = jnp.zeros_like(slab)
            pair = jnp.concatenate([jnp.where(low, slab, zero), jnp.where(low, zero, slab)], axis=0)
            fresh_k = kv_all[g, :, :, k_span].reshape(n_seq * rows, SLAB)
            fresh_v = kv_all[g, :, :, v_span].reshape(n_seq * rows, SLAB)
            stale_k = stale_all[:, g, :, k_span].reshape(n_seq * stale_rows, SLAB)
            stale_v = stale_all[:, g, :, v_span].reshape(n_seq * stale_rows, SLAB)
            s_f = lax.dot_general(pair, fresh_k, contract_last, preferred_element_type=F32) + bias_f[...]
            s_s = lax.dot_general(pair, stale_k, contract_last, preferred_element_type=F32) + bias_s[...]
            top = jnp.maximum(jnp.max(s_f, axis=-1, keepdims=True), jnp.max(s_s, axis=-1, keepdims=True))
            e_f = jnp.exp(s_f - top)
            e_s = jnp.exp(s_s - top)
            total = jnp.sum(e_f, axis=-1, keepdims=True) + jnp.sum(e_s, axis=-1, keepdims=True)
            mixed = jnp.dot(e_f.astype(BF16), fresh_v, preferred_element_type=F32)
            mixed = mixed + jnp.dot(e_s.astype(BF16), stale_v, preferred_element_type=F32)
            mixed = mixed / total
            attended[:, span] = jnp.where(low, mixed[:rows], mixed[rows:]).astype(BF16)

    def part_copy(k):
        return pltpu.make_async_remote_copy(
            src_ref=part_send.at[k], dst_ref=part_recv.at[k], send_sem=p_send.at[k],
            recv_sem=p_recv.at[k], device_id=at(section, seq, lax.rem(mp + k, n_mp)), device_id_type=MESH)

    weight_copies[-1].wait()

    def out_block(j):
        return jnp.dot(attended[...], w_out[:, block(j)], preferred_element_type=F32)

    for k in range(1, n_mp):
        part_send[k] = out_block(lax.rem(mp + k, n_mp)).astype(BF16)
        part_copy(k).start()
    summed = out_block(mp)
    for k in range(1, n_mp):
        part_copy(k).wait_recv()
        summed = summed + part_recv[k].astype(F32)
    gate_at = 2 * n_mp + mp
    gate = mod_all[gate_at // 3, 0:1, pl.ds(pl.multiple_of(gate_at % 3 * cols, SLAB), cols)]
    result[:, block(mp)] = (x_buf[:, block(mp)].astype(F32) + gate * summed).astype(BF16)

    def result_copy(k, origin):
        return pltpu.make_async_remote_copy(
            src_ref=result.at[:, block(origin)], dst_ref=result.at[:, block(origin)], send_sem=res_send.at[k],
            recv_sem=res_recv.at[k], device_id=at(section, seq, lax.rem(mp + k, n_mp)), device_id_type=MESH)

    @pl.when(section == 0)
    def _():
        cross_copy().start()

    for k in range(1, n_mp):
        result_copy(k, mp).start()
    for k in range(1, n_mp):
        result_copy(k, lax.rem(mp + n_mp - k, n_mp)).wait_recv()
    hidden_video[...] = result[pl.ds(0, video_rows)]
    hidden_text[...] = result[pl.ds(video_rows, rows - video_rows)]

    @pl.when(section == 0)
    def _():
        cross_copy().wait_send()

    @pl.when(section == 1)
    def _():
        for k in range(1, n_mp):
            forward_copy(k, mp).wait_send()

    for k in range(1, n_mp):
        mod_copy(k).wait_send()
        part_copy(k).wait_send()
        result_copy(k, mp).wait_send()
    for k in range(1, n_seq):
        stale_copy(k, seq).wait_send()
        for g in range(groups):
            kv_copy(g, k, seq).wait_send()


def body(video, text, patch_lengths, text_len, timestep, w_mod, w_qkv, w_out, stale_cache):
    n_seq, n_mp = lax.axis_size("seq"), lax.axis_size("mp")
    requests, patches, per_dev, width = video.shape
    text_dev = text.shape[1]
    cols = w_out.shape[1]
    groups = cols // GROUP
    rows = requests * (patches * per_dev + text_dev)
    video_rows = requests * patches * per_dev
    text_rows = requests * text_dev
    stale_rows = requests * (patches - 1) * per_dev

    half_width = w_mod.shape[1] // 2
    frequency = jnp.exp(-math.log(10000.0) * jnp.arange(half_width, dtype=F32) / half_width)
    phases = timestep.astype(F32)[0] * frequency
    embedding = jnp.concatenate([jnp.cos(phases), jnp.sin(phases)])
    active = jax.nn.silu(embedding).astype(BF16)
    active = jnp.broadcast_to(active[None, :], (16, 2 * half_width))

    stale = stale_cache[0, :, 1:].reshape(stale_rows, 2, groups, GROUP)
    stale = stale.transpose(2, 0, 1, 3).reshape(groups, stale_rows, 2 * GROUP)

    mod_cols = w_mod.shape[2]
    dims = (requests, patches, per_dev, text_dev, n_seq, n_mp, width, cols)
    vmem = pl.BlockSpec(memory_space=pltpu.VMEM)
    smem = pl.BlockSpec(memory_space=pltpu.SMEM)
    hbm = pl.BlockSpec(memory_space=pl.ANY)
    dma = pltpu.SemaphoreType.DMA
    hidden_video, hidden_text, cache_video, cache_text = pl.pallas_call(
        functools.partial(kernel, dims),
        out_shape=(
            jax.ShapeDtypeStruct((video_rows, width), BF16),
            jax.ShapeDtypeStruct((text_rows, width), BF16),
            jax.ShapeDtypeStruct((video_rows, 2 * cols), BF16),
            jax.ShapeDtypeStruct((text_rows, 2 * cols), BF16),
        ),
        in_specs=[smem, smem, vmem, vmem, vmem, vmem, hbm, hbm, hbm],
        out_specs=(vmem,) * 4,
        scratch_shapes=[
            pltpu.VMEM(w_mod.shape[1:], BF16),
            pltpu.VMEM((3, width, cols), BF16),
            pltpu.VMEM((cols, width), BF16),
            pltpu.VMEM((rows, width), BF16),
            pltpu.VMEM((rows, width), BF16),
            pltpu.VMEM((rows, cols), BF16),
            pltpu.VMEM((rows, cols), BF16),
            pltpu.VMEM((rows, width), BF16),
            pltpu.VMEM((n_mp, 16, mod_cols), F32),
            pltpu.VMEM((groups, n_seq, rows, 2 * GROUP), BF16),
            pltpu.VMEM((n_seq, groups, stale_rows, 2 * GROUP), BF16),
            pltpu.VMEM((n_mp, rows, cols), BF16),
            pltpu.VMEM((n_mp, rows, cols), BF16),
            pltpu.VMEM((2 * rows, n_seq * rows), F32),
            pltpu.VMEM((2 * rows, n_seq * stale_rows), F32),
            dma((11,)),
            dma((n_mp,)), dma((n_mp,)),
            dma((n_seq,)), dma((n_seq,)),
            dma((groups, n_seq)), dma((groups, n_seq)),
            dma((n_mp,)), dma((n_mp,)),
            dma, dma((n_mp,)), dma((n_mp,)),
            dma((n_mp,)), dma((n_mp,)),
        ],
        compiler_params=pltpu.CompilerParams(
            collective_id=0, has_side_effects=True, vmem_limit_bytes=56 * 1024 * 1024
        ),
        cost_estimate=pl.CostEstimate(
            flops=2 * rows * width * 4 * cols, bytes_accessed=2 * width * (4 * cols + 2 * half_width), transcendentals=0
        ),
        name="layer",
    )(
        patch_lengths, text_len, active,
        video.reshape(video_rows, width), text.reshape(text_rows, width), stale,
        w_mod[0], w_qkv[0].transpose(1, 0, 2), w_out[0],
    )
    return (
        hidden_video.reshape(1, requests, patches, per_dev, width),
        hidden_text.reshape(1, requests, text_dev, width),
        cache_video.reshape(1, requests, patches, per_dev, 2, cols),
        cache_text.reshape(1, requests, text_dev, 2, cols),
    )


def solution(mesh):
    placed = (
        P(None, None, "seq", None),
        P(None, "seq", None),
        P(),
        P(),
        P(),
        P("section", None, "mp"),
        P("section", None, None, "mp"),
        P("section", "mp", None),
        P("section", None, None, "seq", None, "mp"),
    )
    return jax.shard_map(
        body,
        mesh=mesh,
        in_specs=placed,
        out_specs=(
            P("section", None, None, "seq", None),
            P("section", None, "seq", None),
            P("section", None, None, "seq", None, "mp"),
            P("section", None, "seq", None, "mp"),
        ),
        check_vma=False,
    )
```

```python
import functools
import math

import jax
import jax.numpy as jnp
from jax import lax
from jax.experimental import pallas as pl
from jax.experimental.pallas import tpu as pltpu
from jax.sharding import PartitionSpec as P

HEAD = 64
EPS = 1e-05
NEG = -1e30
SLAB = 128
GROUP = 256
MESH = pl.DeviceIdType.MESH
F32 = jnp.float32
BF16 = jnp.bfloat16


def slot_marks(index, lengths_ref, text_ref, requests, first, patches, per_dev, text_dev, owner):
    req = jnp.zeros_like(index)
    patch = jnp.zeros_like(index)
    limit = jnp.zeros_like(index)
    start = jnp.zeros_like(index)
    at = 0
    for r in range(requests):
        for p in range(first, patches):
            inside = (index >= at) & (index < at + per_dev)
            req = jnp.where(inside, r, req)
            patch = jnp.where(inside, p, patch)
            limit = jnp.where(inside, lengths_ref[r, p], limit)
            start = jnp.where(inside, at, start)
            at += per_dev
    width = jnp.full_like(index, per_dev)
    for r in range(requests if text_dev else 0):
        inside = (index >= at) & (index < at + text_dev)
        req = jnp.where(inside, r, req)
        limit = jnp.where(inside, text_ref[r], limit)
        start = jnp.where(inside, at, start)
        width = jnp.where(inside, text_dev, width)
        at += text_dev
    live = owner * width + index - start < limit
    return req, patch, live


def split_index(shape, dim, size, count):
    index = lax.broadcasted_iota(jnp.int32, shape, dim)
    owner = jnp.zeros_like(index)
    for j in range(1, count):
        owner = owner + jnp.where(index >= j * size, 1, 0)
    return owner, index - owner * size


def kernel(dims, lengths_ref, text_len_ref, act_ref, video_ref, text_ref, stale_ref, w_mod_hbm,
           w_qkv_hbm, w_out_hbm, hidden_video, hidden_text, cache_video, cache_text,
           w_mod, w_qkv, w_out, x_buf, normed, query, attended, result, mod_all, kv_all, stale_all,
           part_send, part_recv, bias_f, bias_s,
           w_sem, mod_send, mod_recv, stale_send, stale_recv, kv_send, kv_recv, p_send, p_recv,
           cross_send, cross_recv, x_send, x_recv, res_send, res_recv):
    requests, patches, per_dev, text_dev, n_seq, n_mp, width, cols = dims
    rows = requests * (patches * per_dev + text_dev)
    video_rows = requests * patches * per_dev
    stale_rows = requests * (patches - 1) * per_dev
    groups = cols // GROUP
    section = lax.axis_index("section")
    seq = lax.axis_index("seq")
    mp = lax.axis_index("mp")
    other = 1 - section
    core_mate = mp + 1 - 2 * lax.rem(mp, 2)
    y_mate = lax.rem(mp + 2, n_mp)
    diagonal = lax.rem(core_mate + 2, n_mp)
    half = rows // 32 * 16 + 16 * (rows // 16 % 2)
    row_pieces = (pl.ds(0, half), pl.ds(half, rows - half))

    def at(sec, se, m):
        return (sec, se, m)

    weight_copies = [pltpu.make_async_copy(w_mod_hbm, w_mod, w_sem.at[0])]
    pieces = 3
    piece = width // pieces
    for part in (1, 2, 0):
        for i in range(pieces):
            weight_copies.append(pltpu.make_async_copy(
                w_qkv_hbm.at[part, pl.ds(i * piece, piece)],
                w_qkv.at[part, pl.ds(i * piece, piece)],
                w_sem.at[1 + part * pieces + i]))
    weight_copies.append(pltpu.make_async_copy(w_out_hbm, w_out, w_sem.at[1 + 3 * pieces]))
    for copy in weight_copies:
        copy.start()

    barrier = pltpu.get_barrier_semaphore()
    for k in range(1, n_mp):
        pl.semaphore_signal(barrier, inc=1, device_id=at(section, seq, lax.rem(mp + k, n_mp)), device_id_type=MESH)
    for k in range(1, n_seq):
        pl.semaphore_signal(barrier, inc=1, device_id=at(section, lax.rem(seq + k, n_seq), mp), device_id_type=MESH)
    pl.semaphore_signal(barrier, inc=1, device_id=at(other, seq, mp), device_id_type=MESH)

    weight_copies[0].wait()
    active = jnp.broadcast_to(act_ref[...].astype(F32), (8, act_ref.shape[1])).astype(BF16)
    mod_all[mp] = jnp.dot(active, w_mod[...], preferred_element_type=F32)
    span_all = patches * per_dev
    for kind in range(2):
        whole = stale_ref[:, kind, :].astype(F32)
        kept = jnp.concatenate(
            [whole[r * span_all + per_dev:(r + 1) * span_all] for r in range(requests)], axis=0).astype(BF16)
        for g in range(groups):
            stale_all[seq, g, :, kind * GROUP:(kind + 1) * GROUP] = kept[:, g * GROUP:(g + 1) * GROUP]
    pl.semaphore_wait(barrier, n_mp - 1 + n_seq - 1 + 1)

    def mod_copy(k):
        return pltpu.make_async_remote_copy(
            src_ref=mod_all.at[mp], dst_ref=mod_all.at[mp], send_sem=mod_send.at[k],
            recv_sem=mod_recv.at[k], device_id=at(section, seq, lax.rem(mp + k, n_mp)), device_id_type=MESH)

    def mod_arrival(k):
        origin = lax.rem(mp + n_mp - k, n_mp)
        return pltpu.make_async_remote_copy(
            src_ref=mod_all.at[origin], dst_ref=mod_all.at[origin], send_sem=mod_send.at[k],
            recv_sem=mod_recv.at[k], device_id=at(section, seq, origin), device_id_type=MESH)

    def stale_copy(k, origin):
        return pltpu.make_async_remote_copy(
            src_ref=stale_all.at[origin], dst_ref=stale_all.at[origin], send_sem=stale_send.at[k],
            recv_sem=stale_recv.at[k], device_id=at(section, lax.rem(seq + k, n_seq), mp), device_id_type=MESH)

    for k in range(1, n_mp):
        mod_copy(k).start()
    for k in range(1, n_seq):
        stale_copy(k, seq).start()

    row_head, row_index = split_index((2 * rows, 1), 0, rows, 2)
    row_req, row_patch, _ = slot_marks(
        row_index, lengths_ref, text_len_ref, requests, 0, patches, per_dev, text_dev, row_head)
    key_owner, key_index = split_index((1, n_seq * rows), 1, rows, n_seq)
    key_req, key_patch, key_live = slot_marks(
        key_index, lengths_ref, text_len_ref, requests, 0, patches, per_dev, text_dev, key_owner)
    key_limit = jnp.where(key_live, key_patch, patches)
    bias_f[...] = jnp.where((row_req == key_req) & (key_limit <= row_patch), 0.0, NEG)
    key_owner, key_index = split_index((1, n_seq * stale_rows), 1, stale_rows, n_seq)
    key_req, key_patch, key_live = slot_marks(
        key_index, lengths_ref, text_len_ref, requests, 1, patches, per_dev, 0, key_owner)
    key_limit = jnp.where(key_live, key_patch, -1)
    bias_s[...] = jnp.where((row_req == key_req) & (key_limit > row_patch), 0.0, NEG)

    @pl.when(section == 0)
    def _():
        x_buf[pl.ds(0, video_rows)] = video_ref[...]
        x_buf[pl.ds(video_rows, rows - video_rows)] = text_ref[...]

    def block(j):
        return pl.ds(pl.multiple_of(j * cols, SLAB), cols)

    def cross_copy(c):
        return pltpu.make_async_remote_copy(
            src_ref=result.at[row_pieces[c], block(mp)], dst_ref=x_buf.at[row_pieces[c], block(mp)],
            send_sem=cross_send.at[c], recv_sem=cross_recv.at[c], device_id=at(other, seq, mp), device_id_type=MESH)

    def spread_copy(buffer, sems, c, kind, origin):
        part = buffer.at[row_pieces[c], block(origin)]
        return pltpu.make_async_remote_copy(
            src_ref=part, dst_ref=part, send_sem=sems[0].at[c, kind], recv_sem=sems[1].at[c, kind],
            device_id=at(section, seq, y_mate if kind == 1 else core_mate), device_id_type=MESH)

    def spread_start(buffer, sems, c):
        spread_copy(buffer, sems, c, 1, mp).start()
        spread_copy(buffer, sems, c, 0, mp).start()

    def spread_finish(buffer, sems):
        for c in range(2):
            spread_copy(buffer, sems, c, 1, y_mate).wait_recv()
            spread_copy(buffer, sems, c, 2, y_mate).start()
        for c in range(2):
            spread_copy(buffer, sems, c, 0, core_mate).wait_recv()
            spread_copy(buffer, sems, c, 2, diagonal).wait_recv()

    def spread_sent(buffer, sems):
        for c in range(2):
            for kind, origin in enumerate((mp, mp, y_mate)):
                spread_copy(buffer, sems, c, kind, origin).wait_send()

    x_sems, result_sems = (x_send, x_recv), (res_send, res_recv)

    for k in range(1, n_mp):
        mod_arrival(k).wait_recv()

    @pl.when(section == 1)
    def _():
        for c in range(2):
            cross_copy(c).wait_recv()
            spread_start(x_buf, x_sems, c)
        spread_finish(x_buf, x_sems)

    def modulated(b):
        return mod_all[b // 3, 0:1, (b % 3) * cols:(b % 3 + 1) * cols]

    values = x_buf[...].astype(F32)
    mean = jnp.mean(values, axis=-1, keepdims=True)
    center = values - mean
    inverse = lax.rsqrt(jnp.mean(center * center, axis=-1, keepdims=True) + EPS)
    for c in range(n_mp):
        span = slice(c * cols, (c + 1) * cols)
        piece_values = (x_buf[:, span].astype(F32) - mean) * inverse
        normed[:, span] = (piece_values * (1.0 + modulated(n_mp + c)) + modulated(c)).astype(BF16)

    def kv_copy(g, k, origin):
        return pltpu.make_async_remote_copy(
            src_ref=kv_all.at[g, origin], dst_ref=kv_all.at[g, origin], send_sem=kv_send.at[g, k],
            recv_sem=kv_recv.at[g, k], device_id=at(section, lax.rem(seq + k, n_seq), mp), device_id_type=MESH)

    def project(part, g):
        return jnp.dot(normed[...], w_qkv[part, :, g * GROUP:(g + 1) * GROUP], preferred_element_type=F32)

    for copy in weight_copies[1:1 + pieces]:
        copy.wait()
    for g in range(groups):
        key = project(1, g).astype(BF16)
        if g == 0:
            for copy in weight_copies[1 + pieces:1 + 2 * pieces]:
                copy.wait()
        value = project(2, g).astype(BF16)
        kv_all[g, seq, :, 0:GROUP] = key
        kv_all[g, seq, :, GROUP:2 * GROUP] = value
        for k in range(1, n_seq):
            kv_copy(g, k, seq).start()
    for copy in weight_copies[1 + 2 * pieces:1 + 3 * pieces]:
        copy.wait()
    for g in range(groups):
        query[:, g * GROUP:(g + 1) * GROUP] = (project(0, g).astype(BF16).astype(F32) * HEAD ** (-0.5)).astype(BF16)

    for g in range(groups):
        for kind in range(2):
            span = slice(g * GROUP, (g + 1) * GROUP)
            part = kv_all[g, seq, :, kind * GROUP:(kind + 1) * GROUP]
            cache_video[:, kind, span] = part[:video_rows]
            cache_text[:, kind, span] = part[video_rows:]

    for k in range(1, n_seq):
        stale_copy(k, lax.rem(seq + n_seq - k, n_seq)).wait_recv()
    low = lax.broadcasted_iota(jnp.int32, (rows, SLAB), 1) < HEAD
    contract_last = (((1,), (1,)), ((), ()))
    for g in range(groups):
        for k in range(1, n_seq):
            kv_copy(g, k, lax.rem(seq + n_seq - k, n_seq)).wait_recv()
        for h in range(GROUP // SLAB):
            span = slice(g * GROUP + h * SLAB, g * GROUP + (h + 1) * SLAB)
            k_span = slice(h * SLAB, (h + 1) * SLAB)
            v_span = slice(GROUP + h * SLAB, GROUP + (h + 1) * SLAB)
            slab = query[:, span]
            zero = jnp.zeros_like(slab)
            pair = jnp.concatenate([jnp.where(low, slab, zero), jnp.where(low, zero, slab)], axis=0)
            fresh_k = kv_all[g, :, :, k_span].reshape(n_seq * rows, SLAB)
            fresh_v = kv_all[g, :, :, v_span].reshape(n_seq * rows, SLAB)
            stale_k = stale_all[:, g, :, k_span].reshape(n_seq * stale_rows, SLAB)
            stale_v = stale_all[:, g, :, v_span].reshape(n_seq * stale_rows, SLAB)
            s_f = lax.dot_general(pair, fresh_k, contract_last, preferred_element_type=F32) + bias_f[...]
            s_s = lax.dot_general(pair, stale_k, contract_last, preferred_element_type=F32) + bias_s[...]
            top = jnp.maximum(jnp.max(s_f, axis=-1, keepdims=True), jnp.max(s_s, axis=-1, keepdims=True))
            e_f = jnp.exp(s_f - top)
            e_s = jnp.exp(s_s - top)
            total = jnp.sum(e_f, axis=-1, keepdims=True) + jnp.sum(e_s, axis=-1, keepdims=True)
            mixed = jnp.dot(e_f.astype(BF16), fresh_v, preferred_element_type=F32)
            mixed = mixed + jnp.dot(e_s.astype(BF16), stale_v, preferred_element_type=F32)
            mixed = mixed / total
            attended[:, span] = jnp.where(low, mixed[:rows], mixed[rows:]).astype(BF16)

    def part_copy(k):
        return pltpu.make_async_remote_copy(
            src_ref=part_send.at[k], dst_ref=part_recv.at[k], send_sem=p_send.at[k], recv_sem=p_recv.at[k],
            device_id=at(section, seq, y_mate if k == 2 else core_mate), device_id_type=MESH)

    weight_copies[-1].wait()

    def out_block(j):
        return jnp.dot(attended[...], w_out[:, block(j)], preferred_element_type=F32)

    part_send[0] = out_block(diagonal).astype(BF16)
    part_copy(0).start()
    passed = out_block(y_mate)
    part_copy(0).wait_recv()
    part_send[2] = (passed + part_recv[0].astype(F32)).astype(BF16)
    part_copy(2).start()
    part_send[1] = out_block(core_mate).astype(BF16)
    part_copy(1).start()
    summed = out_block(mp)
    part_copy(1).wait_recv()
    summed = summed + part_recv[1].astype(F32)
    part_copy(2).wait_recv()
    summed = summed + part_recv[2].astype(F32)
    gate_at = 2 * n_mp + mp
    gate = mod_all[gate_at // 3, 0:1, pl.ds(pl.multiple_of(gate_at % 3 * cols, SLAB), cols)]
    result[:, block(mp)] = (x_buf[:, block(mp)].astype(F32) + gate * summed).astype(BF16)

    @pl.when(section == 0)
    def _():
        for c in range(2):
            cross_copy(c).start()

    for c in range(2):
        spread_start(result, result_sems, c)
    spread_finish(result, result_sems)
    hidden_video[...] = result[pl.ds(0, video_rows)]
    hidden_text[...] = result[pl.ds(video_rows, rows - video_rows)]

    @pl.when(section == 0)
    def _():
        for c in range(2):
            cross_copy(c).wait_send()

    @pl.when(section == 1)
    def _():
        spread_sent(x_buf, x_sems)

    spread_sent(result, result_sems)
    for k in range(1, n_mp):
        mod_copy(k).wait_send()
    for k in range(3):
        part_copy(k).wait_send()
    for k in range(1, n_seq):
        stale_copy(k, seq).wait_send()
        for g in range(groups):
            kv_copy(g, k, seq).wait_send()


def store_kernel(*refs):
    sems = refs[-1]
    copies = [pltpu.make_async_copy(refs[i], refs[4 + i], sems.at[i]) for i in range(4)]
    for copy in copies:
        copy.start()
    for copy in copies:
        copy.wait()


def body(video, text, patch_lengths, text_len, timestep, w_mod, w_qkv, w_out, stale_cache):
    n_seq, n_mp = lax.axis_size("seq"), lax.axis_size("mp")
    requests, patches, per_dev, width = video.shape
    text_dev = text.shape[1]
    cols = w_out.shape[1]
    groups = cols // GROUP
    rows = requests * (patches * per_dev + text_dev)
    video_rows = requests * patches * per_dev
    text_rows = requests * text_dev
    stale_rows = requests * (patches - 1) * per_dev

    half_width = w_mod.shape[1] // 2
    frequency = jnp.exp(-math.log(10000.0) * jnp.arange(half_width, dtype=F32) / half_width)
    phases = timestep.astype(F32)[0] * frequency
    embedding = jnp.concatenate([jnp.cos(phases), jnp.sin(phases)])
    active = jax.nn.silu(embedding).astype(BF16)

    mod_cols = w_mod.shape[2]
    dims = (requests, patches, per_dev, text_dev, n_seq, n_mp, width, cols)
    vmem = pl.BlockSpec(memory_space=pltpu.VMEM)
    smem = pl.BlockSpec(memory_space=pltpu.SMEM)
    hbm = pl.BlockSpec(memory_space=pl.ANY)
    dma = pltpu.SemaphoreType.DMA
    outputs = pl.pallas_call(
        functools.partial(kernel, dims),
        out_shape=(
            jax.ShapeDtypeStruct((video_rows, width), BF16),
            jax.ShapeDtypeStruct((text_rows, width), BF16),
            jax.ShapeDtypeStruct((video_rows, 2, cols), BF16),
            jax.ShapeDtypeStruct((text_rows, 2, cols), BF16),
        ),
        in_specs=[smem, smem, vmem, vmem, vmem, vmem, hbm, hbm, hbm],
        out_specs=(vmem,) * 4,
        scratch_shapes=[
            pltpu.VMEM(w_mod.shape[1:], BF16),
            pltpu.VMEM((3, width, cols), BF16),
            pltpu.VMEM((cols, width), BF16),
            pltpu.VMEM((rows, width), BF16),
            pltpu.VMEM((rows, width), BF16),
            pltpu.VMEM((rows, cols), BF16),
            pltpu.VMEM((rows, cols), BF16),
            pltpu.VMEM((rows, width), BF16),
            pltpu.VMEM((n_mp, 8, mod_cols), F32),
            pltpu.VMEM((groups, n_seq, rows, 2 * GROUP), BF16),
            pltpu.VMEM((n_seq, groups, stale_rows, 2 * GROUP), BF16),
            pltpu.VMEM((3, rows, cols), BF16),
            pltpu.VMEM((3, rows, cols), BF16),
            pltpu.VMEM((2 * rows, n_seq * rows), F32),
            pltpu.VMEM((2 * rows, n_seq * stale_rows), F32),
            dma((11,)),
            dma((n_mp,)), dma((n_mp,)),
            dma((n_seq,)), dma((n_seq,)),
            dma((groups, n_seq)), dma((groups, n_seq)),
            dma((n_mp,)), dma((n_mp,)),
            dma((2,)), dma((2,)),
            dma((2, 3)), dma((2, 3)),
            dma((2, 3)), dma((2, 3)),
        ],
        compiler_params=pltpu.CompilerParams(
            collective_id=0, has_side_effects=True, vmem_limit_bytes=56 * 1024 * 1024
        ),
        cost_estimate=pl.CostEstimate(
            flops=2 * rows * width * 4 * cols, bytes_accessed=2 * width * (4 * cols + 2 * half_width), transcendentals=0
        ),
        name="layer",
    )(
        patch_lengths, text_len, active[None, :],
        video.reshape(video_rows, width), text.reshape(text_rows, width), stale_cache.reshape(video_rows, 2, cols),
        w_mod[0], w_qkv[0].transpose(1, 0, 2), w_out[0],
    )
    hidden_video, hidden_text, cache_video, cache_text = pl.pallas_call(
        store_kernel,
        out_shape=tuple(jax.ShapeDtypeStruct(o.shape, o.dtype) for o in outputs),
        in_specs=[hbm] * 4,
        out_specs=(hbm,) * 4,
        scratch_shapes=[dma((4,))],
        compiler_params=pltpu.CompilerParams(vmem_limit_bytes=56 * 1024 * 1024),
        name="store",
    )(*outputs)
    return (
        hidden_video.reshape(1, requests, patches, per_dev, width),
        hidden_text.reshape(1, requests, text_dev, width),
        cache_video.reshape(1, requests, patches, per_dev, 2, cols),
        cache_text.reshape(1, requests, text_dev, 2, cols),
    )


def solution(mesh):
    placed = (
        P(None, None, "seq", None),
        P(None, "seq", None),
        P(),
        P(),
        P(),
        P("section", None, "mp"),
        P("section", None, None, "mp"),
        P("section", "mp", None),
        P("section", None, None, "seq", None, "mp"),
    )
    return jax.shard_map(
        body,
        mesh=mesh,
        in_specs=placed,
        out_specs=(
            P("section", None, None, "seq", None),
            P("section", None, "seq", None),
            P("section", None, None, "seq", None, "mp"),
            P("section", None, "seq", None, "mp"),
        ),
        check_vma=False,
    )
```

```python
import functools
import math

import jax
import jax.numpy as jnp
from jax import lax
from jax.experimental import pallas as pl
from jax.experimental.pallas import tpu as pltpu
from jax.sharding import PartitionSpec as P

HEAD = 64
EPS = 1e-05
NEG = -1e30
SLAB = 128
GROUP = 256
MESH = pl.DeviceIdType.MESH
F32 = jnp.float32
BF16 = jnp.bfloat16


def slot_marks(index, lengths_ref, text_ref, requests, first, patches, per_dev, text_dev, owner):
    req = jnp.zeros_like(index)
    patch = jnp.zeros_like(index)
    limit = jnp.zeros_like(index)
    start = jnp.zeros_like(index)
    at = 0
    for r in range(requests):
        for p in range(first, patches):
            inside = (index >= at) & (index < at + per_dev)
            req = jnp.where(inside, r, req)
            patch = jnp.where(inside, p, patch)
            limit = jnp.where(inside, lengths_ref[r, p], limit)
            start = jnp.where(inside, at, start)
            at += per_dev
    width = jnp.full_like(index, per_dev)
    for r in range(requests if text_dev else 0):
        inside = (index >= at) & (index < at + text_dev)
        req = jnp.where(inside, r, req)
        limit = jnp.where(inside, text_ref[r], limit)
        start = jnp.where(inside, at, start)
        width = jnp.where(inside, text_dev, width)
        at += text_dev
    live = owner * width + index - start < limit
    return req, patch, live


def split_index(shape, dim, size, count):
    index = lax.broadcasted_iota(jnp.int32, shape, dim)
    owner = jnp.zeros_like(index)
    for j in range(1, count):
        owner = owner + jnp.where(index >= j * size, 1, 0)
    return owner, index - owner * size


def kernel(dims, lengths_ref, text_len_ref, act_ref, video_ref, text_ref, stale_ref, w_mod_hbm,
           w_qkv_hbm, w_out_hbm, hidden_video, hidden_text, cache_video, cache_text,
           w_mod, w_qkv, w_out, x_buf, normed, projected, attended, result, mod_all, heads_send, heads_recv,
           back_send, back_recv, stale_send_buf, stale_recv_buf, key_cat, value_cat, part_send, part_recv, bias,
           w_sem, mod_send, mod_recv, stale_send, stale_recv, heads_out, heads_in, back_out, back_in, p_send, p_recv,
           cross_send, cross_recv, x_send, x_recv, res_send, res_recv):
    requests, patches, per_dev, text_dev, n_seq, n_mp, width, cols = dims
    rows = requests * (patches * per_dev + text_dev)
    video_rows = requests * patches * per_dev
    stale_rows = requests * (patches - 1) * per_dev
    groups = cols // GROUP
    each, active = head_split(cols // HEAD, n_seq)
    share = each * HEAD
    fresh_keys = n_seq * rows
    section = lax.axis_index("section")
    seq = lax.axis_index("seq")
    mp = lax.axis_index("mp")
    other = 1 - section
    core_mate = mp + 1 - 2 * lax.rem(mp, 2)
    y_mate = lax.rem(mp + 2, n_mp)
    diagonal = lax.rem(core_mate + 2, n_mp)
    half = rows // 32 * 16 + 16 * (rows // 16 % 2)
    row_pieces = (pl.ds(0, half), pl.ds(half, rows - half))

    def at(sec, se, m):
        return (sec, se, m)

    weight_copies = [pltpu.make_async_copy(w_mod_hbm, w_mod, w_sem.at[0])]
    pieces = 3
    piece = width // pieces
    for part in (1, 2, 0):
        for i in range(pieces):
            weight_copies.append(pltpu.make_async_copy(
                w_qkv_hbm.at[part, pl.ds(i * piece, piece)],
                w_qkv.at[part, pl.ds(i * piece, piece)],
                w_sem.at[1 + part * pieces + i]))
    weight_copies.append(pltpu.make_async_copy(w_out_hbm, w_out, w_sem.at[1 + 3 * pieces]))
    for copy in weight_copies:
        copy.start()

    barrier = pltpu.get_barrier_semaphore()
    for k in range(1, n_mp):
        pl.semaphore_signal(barrier, inc=1, device_id=at(section, seq, lax.rem(mp + k, n_mp)), device_id_type=MESH)
    for k in range(1, n_seq):
        pl.semaphore_signal(barrier, inc=1, device_id=at(section, lax.rem(seq + k, n_seq), mp), device_id_type=MESH)
    pl.semaphore_signal(barrier, inc=1, device_id=at(other, seq, mp), device_id_type=MESH)

    weight_copies[0].wait()
    act = jnp.broadcast_to(act_ref[...].astype(F32), (8, act_ref.shape[1])).astype(BF16)
    mod_all[mp] = jnp.dot(act, w_mod[...], preferred_element_type=F32)
    span_all = patches * per_dev
    for kind in range(2):
        whole = stale_ref[:, kind, :].astype(F32)
        kept = jnp.concatenate(
            [whole[r * span_all + per_dev:(r + 1) * span_all] for r in range(requests)], axis=0).astype(BF16)
        for d in range(active):
            stale_send_buf[d, :, kind * share:(kind + 1) * share] = kept[:, d * share:(d + 1) * share]
    pl.semaphore_wait(barrier, n_mp - 1 + n_seq - 1 + 1)

    def mod_copy(k):
        return pltpu.make_async_remote_copy(
            src_ref=mod_all.at[mp], dst_ref=mod_all.at[mp], send_sem=mod_send.at[k],
            recv_sem=mod_recv.at[k], device_id=at(section, seq, lax.rem(mp + k, n_mp)), device_id_type=MESH)

    def mod_arrival(k):
        origin = lax.rem(mp + n_mp - k, n_mp)
        return pltpu.make_async_remote_copy(
            src_ref=mod_all.at[origin], dst_ref=mod_all.at[origin], send_sem=mod_send.at[k],
            recv_sem=mod_recv.at[k], device_id=at(section, seq, origin), device_id_type=MESH)

    def to_device(send, recv, sems, d):
        return pltpu.make_async_remote_copy(
            src_ref=send.at[d], dst_ref=recv.at[seq], send_sem=sems[0].at[d], recv_sem=sems[1].at[seq],
            device_id=at(section, d, mp), device_id_type=MESH)

    def from_device(send, recv, sems, origin):
        return pltpu.make_async_remote_copy(
            src_ref=recv.at[origin], dst_ref=recv.at[origin], send_sem=sems[0].at[origin], recv_sem=sems[1].at[origin],
            device_id=at(section, origin, mp), device_id_type=MESH)

    def send_part(exchange, d):
        @pl.when(seq != d)
        def _():
            to_device(*exchange, d).start()

    def keep_part(exchange, d):
        @pl.when(seq == d)
        def _():
            exchange[1][d] = exchange[0][d]

    def sent_part(exchange, d):
        @pl.when(seq != d)
        def _():
            to_device(*exchange, d).wait_send()

    stale_exchange = (stale_send_buf, stale_recv_buf, (stale_send, stale_recv))
    heads_exchange = (heads_send, heads_recv, (heads_out, heads_in))
    back_exchange = (back_send, back_recv, (back_out, back_in))

    def when_active(function):
        if active == n_seq:
            function()
        else:
            pl.when(seq < active)(function)

    for k in range(1, n_mp):
        mod_copy(k).start()
    for d in range(active):
        send_part(stale_exchange, d)
        keep_part(stale_exchange, d)

    row_index = lax.broadcasted_iota(jnp.int32, (rows, 1), 0)
    row_req, row_patch, _ = slot_marks(
        row_index, lengths_ref, text_len_ref, requests, 0, patches, per_dev, text_dev, 0)
    key_owner, key_index = split_index((1, n_seq * rows), 1, rows, n_seq)
    key_req, key_patch, key_live = slot_marks(
        key_index, lengths_ref, text_len_ref, requests, 0, patches, per_dev, text_dev, key_owner)
    key_limit = jnp.where(key_live, key_patch, patches)
    bias[:, :fresh_keys] = jnp.where((row_req == key_req) & (key_limit <= row_patch), 0.0, NEG)
    key_owner, key_index = split_index((1, n_seq * stale_rows), 1, stale_rows, n_seq)
    key_req, key_patch, key_live = slot_marks(
        key_index, lengths_ref, text_len_ref, requests, 1, patches, per_dev, 0, key_owner)
    key_limit = jnp.where(key_live, key_patch, -1)
    bias[:, fresh_keys:] = jnp.where((row_req == key_req) & (key_limit > row_patch), 0.0, NEG)

    @pl.when(section == 0)
    def _():
        x_buf[pl.ds(0, video_rows)] = video_ref[...]
        x_buf[pl.ds(video_rows, rows - video_rows)] = text_ref[...]

    def block(j):
        return pl.ds(pl.multiple_of(j * cols, SLAB), cols)

    def cross_copy(c):
        return pltpu.make_async_remote_copy(
            src_ref=result.at[row_pieces[c], block(mp)], dst_ref=x_buf.at[row_pieces[c], block(mp)],
            send_sem=cross_send.at[c], recv_sem=cross_recv.at[c], device_id=at(other, seq, mp), device_id_type=MESH)

    def spread_copy(buffer, sems, c, kind, origin):
        part = buffer.at[row_pieces[c], block(origin)]
        return pltpu.make_async_remote_copy(
            src_ref=part, dst_ref=part, send_sem=sems[0].at[c, kind], recv_sem=sems[1].at[c, kind],
            device_id=at(section, seq, y_mate if kind == 1 else core_mate), device_id_type=MESH)

    def spread_start(buffer, sems, c):
        spread_copy(buffer, sems, c, 1, mp).start()
        spread_copy(buffer, sems, c, 0, mp).start()

    def spread_finish(buffer, sems):
        for c in range(2):
            spread_copy(buffer, sems, c, 1, y_mate).wait_recv()
            spread_copy(buffer, sems, c, 2, y_mate).start()
        for c in range(2):
            spread_copy(buffer, sems, c, 0, core_mate).wait_recv()
            spread_copy(buffer, sems, c, 2, diagonal).wait_recv()

    def spread_sent(buffer, sems):
        for c in range(2):
            for kind, origin in enumerate((mp, mp, y_mate)):
                spread_copy(buffer, sems, c, kind, origin).wait_send()

    x_sems, result_sems = (x_send, x_recv), (res_send, res_recv)

    for k in range(1, n_mp):
        mod_arrival(k).wait_recv()

    @pl.when(section == 1)
    def _():
        for c in range(2):
            cross_copy(c).wait_recv()
            spread_start(x_buf, x_sems, c)
        spread_finish(x_buf, x_sems)

    def modulated(b):
        return mod_all[b // 3, 0:1, (b % 3) * cols:(b % 3 + 1) * cols]

    values = x_buf[...].astype(F32)
    mean = jnp.mean(values, axis=-1, keepdims=True)
    center = values - mean
    inverse = lax.rsqrt(jnp.mean(center * center, axis=-1, keepdims=True) + EPS)
    for c in range(n_mp):
        span = slice(c * cols, (c + 1) * cols)
        piece_values = (x_buf[:, span].astype(F32) - mean) * inverse
        normed[:, span] = (piece_values * (1.0 + modulated(n_mp + c)) + modulated(c)).astype(BF16)

    def project(part, g):
        return jnp.dot(normed[...], w_qkv[part, :, g * GROUP:(g + 1) * GROUP], preferred_element_type=F32)

    order = []
    for t in range(groups):
        order.insert(t, groups - 1 - t // 2 if t % 2 else t // 2)
    done, sent = set(), set()
    for g in order:
        for part in (1, 2, 0):
            if g == order[0]:
                at_piece = 1 + (1, 2, 0).index(part) * pieces
                for copy in weight_copies[at_piece:at_piece + pieces]:
                    copy.wait()
            tile = project(part, g).astype(BF16)
            if part == 0:
                tile = (tile.astype(F32) * HEAD ** (-0.5)).astype(BF16)
            projected[part, :, g * GROUP:(g + 1) * GROUP] = tile
        done.add(g)
        for d in range(active):
            first, last = d * share // GROUP, ((d + 1) * share - 1) // GROUP
            if d not in sent and all(t in done for t in range(first, last + 1)):
                sent.add(d)
                for part in range(3):
                    heads_send[d, :, part * share:(part + 1) * share] = projected[part, :, d * share:(d + 1) * share]
                send_part(heads_exchange, d)
                keep_part(heads_exchange, d)

    for g in range(groups):
        for kind in range(2):
            span = slice(g * GROUP, (g + 1) * GROUP)
            part = projected[1 + kind, :, span]
            cache_video[:, kind, span] = part[:video_rows]
            cache_text[:, kind, span] = part[video_rows:]

    @when_active
    def _():
        for k in range(1, n_seq):
            from_device(*stale_exchange, lax.rem(seq + n_seq - k, n_seq)).wait_recv()
        for h in range(each):
            for kind, cat in enumerate((key_cat, value_cat)):
                at_col = kind * share + h * HEAD
                cat[h, fresh_keys:] = stale_recv_buf[:, :, at_col:at_col + HEAD].reshape(n_seq * stale_rows, HEAD)
        for k in range(1, n_seq):
            from_device(*heads_exchange, lax.rem(seq + n_seq - k, n_seq)).wait_recv()
        for h in range(each):
            for kind, cat in enumerate((key_cat, value_cat)):
                at_col = (1 + kind) * share + h * HEAD
                cat[h, :fresh_keys] = heads_recv[:, :, at_col:at_col + HEAD].reshape(fresh_keys, HEAD)
        for i in range(n_seq):
            d = n_seq - 1 - i // 2 if i % 2 else i // 2
            for h in range(each):
                heads_at = slice(h * HEAD, (h + 1) * HEAD)
                scores = lax.dot_general(
                    heads_recv[d, :, heads_at], key_cat[h], (((1,), (1,)), ((), ())), preferred_element_type=F32)
                scores = scores + bias[...]
                top = jnp.max(scores, axis=-1, keepdims=True)
                weights = jnp.exp(scores - top)
                total = jnp.sum(weights, axis=-1, keepdims=True)
                mixed = jnp.dot(weights.astype(BF16), value_cat[h], preferred_element_type=F32)
                back_send[d, :, heads_at] = (mixed / total).astype(BF16)
            send_part(back_exchange, d)
            keep_part(back_exchange, d)

    for d in range(active):
        @pl.when(seq != d)
        def _():
            from_device(*back_exchange, d).wait_recv()
    for d in range(active):
        attended[:, d * share:(d + 1) * share] = back_recv[d, :, :share]

    def part_copy(k):
        return pltpu.make_async_remote_copy(
            src_ref=part_send.at[k], dst_ref=part_recv.at[k], send_sem=p_send.at[k], recv_sem=p_recv.at[k],
            device_id=at(section, seq, y_mate if k == 2 else core_mate), device_id_type=MESH)

    weight_copies[-1].wait()

    def out_block(j):
        return jnp.dot(attended[...], w_out[:, block(j)], preferred_element_type=F32)

    part_send[0] = out_block(diagonal).astype(BF16)
    part_copy(0).start()
    passed = out_block(y_mate)
    part_copy(0).wait_recv()
    part_send[2] = (passed + part_recv[0].astype(F32)).astype(BF16)
    part_copy(2).start()
    part_send[1] = out_block(core_mate).astype(BF16)
    part_copy(1).start()
    summed = out_block(mp)
    part_copy(1).wait_recv()
    summed = summed + part_recv[1].astype(F32)
    part_copy(2).wait_recv()
    summed = summed + part_recv[2].astype(F32)
    gate_at = 2 * n_mp + mp
    gate = mod_all[gate_at // 3, 0:1, pl.ds(pl.multiple_of(gate_at % 3 * cols, SLAB), cols)]
    result[:, block(mp)] = (x_buf[:, block(mp)].astype(F32) + gate * summed).astype(BF16)

    @pl.when(section == 0)
    def _():
        for c in range(2):
            cross_copy(c).start()

    for c in range(2):
        spread_start(result, result_sems, c)
    spread_finish(result, result_sems)
    hidden_video[...] = result[pl.ds(0, video_rows)]
    hidden_text[...] = result[pl.ds(video_rows, rows - video_rows)]

    @pl.when(section == 0)
    def _():
        for c in range(2):
            cross_copy(c).wait_send()

    @pl.when(section == 1)
    def _():
        spread_sent(x_buf, x_sems)

    spread_sent(result, result_sems)
    for k in range(1, n_mp):
        mod_copy(k).wait_send()
    for k in range(3):
        part_copy(k).wait_send()
    for d in range(active):
        sent_part(stale_exchange, d)
        sent_part(heads_exchange, d)

    @when_active
    def _():
        for d in range(n_seq):
            sent_part(back_exchange, d)


def store_kernel(*refs):
    ins, outs, held, sems = refs[:4], refs[4:8], refs[8:12], refs[12]
    loads = [pltpu.make_async_copy(ins[i], held[i], sems.at[0, i]) for i in range(4)]
    stores = [pltpu.make_async_copy(held[i], outs[i], sems.at[1, i]) for i in range(4)]
    for copy in loads:
        copy.start()
    for load, store in zip(loads, stores):
        load.wait()
        store.start()
    for copy in stores:
        copy.wait()


def padded(count):
    return -(-count // SLAB) * SLAB


def head_split(heads, n_seq):
    each = -(-heads // n_seq)
    while heads % each:
        each += 1
    return each, heads // each


def body(video, text, patch_lengths, text_len, timestep, w_mod, w_qkv, w_out, stale_cache):
    n_seq, n_mp = lax.axis_size("seq"), lax.axis_size("mp")
    requests, patches, per_dev, width = video.shape
    text_dev = text.shape[1]
    cols = w_out.shape[1]
    each, active = head_split(cols // HEAD, n_seq)
    share = each * HEAD
    rows = requests * (patches * per_dev + text_dev)
    video_rows = requests * patches * per_dev
    text_rows = requests * text_dev
    stale_rows = requests * (patches - 1) * per_dev

    half_width = w_mod.shape[1] // 2
    frequency = jnp.exp(-math.log(10000.0) * jnp.arange(half_width, dtype=F32) / half_width)
    phases = timestep.astype(F32)[0] * frequency
    embedding = jnp.concatenate([jnp.cos(phases), jnp.sin(phases)])
    act = jax.nn.silu(embedding).astype(BF16)

    mod_cols = w_mod.shape[2]
    keys = n_seq * (rows + stale_rows)
    dims = (requests, patches, per_dev, text_dev, n_seq, n_mp, width, cols)
    vmem = pl.BlockSpec(memory_space=pltpu.VMEM)
    smem = pl.BlockSpec(memory_space=pltpu.SMEM)
    hbm = pl.BlockSpec(memory_space=pl.ANY)
    dma = pltpu.SemaphoreType.DMA
    outputs = pl.pallas_call(
        functools.partial(kernel, dims),
        out_shape=(
            jax.ShapeDtypeStruct((video_rows, width), BF16),
            jax.ShapeDtypeStruct((text_rows, width), BF16),
            jax.ShapeDtypeStruct((video_rows, 2, cols), BF16),
            jax.ShapeDtypeStruct((text_rows, 2, cols), BF16),
        ),
        in_specs=[smem, smem, vmem, vmem, vmem, vmem, hbm, hbm, hbm],
        out_specs=(vmem,) * 4,
        scratch_shapes=[
            pltpu.VMEM(w_mod.shape[1:], BF16),
            pltpu.VMEM((3, width, cols), BF16),
            pltpu.VMEM((cols, width), BF16),
            pltpu.VMEM((rows, width), BF16),
            pltpu.VMEM((rows, width), BF16),
            pltpu.VMEM((3, rows, cols), BF16),
            pltpu.VMEM((rows, cols), BF16),
            pltpu.VMEM((rows, width), BF16),
            pltpu.VMEM((n_mp, 8, mod_cols), F32),
            pltpu.VMEM((active, rows, padded(3 * share)), BF16),
            pltpu.VMEM((n_seq, rows, padded(3 * share)), BF16),
            pltpu.VMEM((n_seq, rows, padded(share)), BF16),
            pltpu.VMEM((n_seq, rows, padded(share)), BF16),
            pltpu.VMEM((active, stale_rows, padded(2 * share)), BF16),
            pltpu.VMEM((n_seq, stale_rows, padded(2 * share)), BF16),
            pltpu.VMEM((each, keys, HEAD), BF16),
            pltpu.VMEM((each, keys, HEAD), BF16),
            pltpu.VMEM((3, rows, cols), BF16),
            pltpu.VMEM((3, rows, cols), BF16),
            pltpu.VMEM((rows, keys), F32),
            dma((11,)),
            dma((n_mp,)), dma((n_mp,)),
            dma((n_seq,)), dma((n_seq,)),
            dma((n_seq,)), dma((n_seq,)),
            dma((n_seq,)), dma((n_seq,)),
            dma((n_mp,)), dma((n_mp,)),
            dma((2,)), dma((2,)),
            dma((2, 3)), dma((2, 3)),
            dma((2, 3)), dma((2, 3)),
        ],
        compiler_params=pltpu.CompilerParams(
            collective_id=0, has_side_effects=True, vmem_limit_bytes=56 * 1024 * 1024
        ),
        cost_estimate=pl.CostEstimate(
            flops=2 * rows * width * 4 * cols, bytes_accessed=2 * width * (4 * cols + 2 * half_width), transcendentals=0
        ),
        name="layer",
    )(
        patch_lengths, text_len, act[None, :],
        video.reshape(video_rows, width), text.reshape(text_rows, width), stale_cache.reshape(video_rows, 2, cols),
        w_mod[0], w_qkv[0].transpose(1, 0, 2), w_out[0],
    )
    hidden_video, hidden_text, cache_video, cache_text = pl.pallas_call(
        store_kernel,
        out_shape=tuple(jax.ShapeDtypeStruct(o.shape, o.dtype) for o in outputs),
        in_specs=[hbm] * 4,
        out_specs=(hbm,) * 4,
        scratch_shapes=[pltpu.VMEM(o.shape, o.dtype) for o in outputs] + [dma((2, 4))],
        compiler_params=pltpu.CompilerParams(vmem_limit_bytes=56 * 1024 * 1024),
        name="store",
    )(*outputs)
    return (
        hidden_video.reshape(1, requests, patches, per_dev, width),
        hidden_text.reshape(1, requests, text_dev, width),
        cache_video.reshape(1, requests, patches, per_dev, 2, cols),
        cache_text.reshape(1, requests, text_dev, 2, cols),
    )


def solution(mesh):
    placed = (
        P(None, None, "seq", None),
        P(None, "seq", None),
        P(),
        P(),
        P(),
        P("section", None, "mp"),
        P("section", None, None, "mp"),
        P("section", "mp", None),
        P("section", None, None, "seq", None, "mp"),
    )
    return jax.shard_map(
        body,
        mesh=mesh,
        in_specs=placed,
        out_specs=(
            P("section", None, None, "seq", None),
            P("section", None, "seq", None),
            P("section", None, None, "seq", None, "mp"),
            P("section", None, "seq", None, "mp"),
        ),
        check_vma=False,
    )
```

```python
import functools
import math

import jax
import jax.numpy as jnp
from jax import lax
from jax.experimental import pallas as pl
from jax.experimental.pallas import tpu as pltpu
from jax.sharding import PartitionSpec as P

HEAD = 64
EPS = 1e-05
NEG = -1e30
SLAB = 128
GROUP = 256
MESH = pl.DeviceIdType.MESH
F32 = jnp.float32
BF16 = jnp.bfloat16


def slot_marks(index, lengths_ref, text_ref, requests, first, patches, per_dev, text_dev, owner):
    req = jnp.zeros_like(index)
    patch = jnp.zeros_like(index)
    limit = jnp.zeros_like(index)
    start = jnp.zeros_like(index)
    at = 0
    for r in range(requests):
        for p in range(first, patches):
            inside = (index >= at) & (index < at + per_dev)
            req = jnp.where(inside, r, req)
            patch = jnp.where(inside, p, patch)
            limit = jnp.where(inside, lengths_ref[r, p], limit)
            start = jnp.where(inside, at, start)
            at += per_dev
    width = jnp.full_like(index, per_dev)
    for r in range(requests if text_dev else 0):
        inside = (index >= at) & (index < at + text_dev)
        req = jnp.where(inside, r, req)
        limit = jnp.where(inside, text_ref[r], limit)
        start = jnp.where(inside, at, start)
        width = jnp.where(inside, text_dev, width)
        at += text_dev
    live = owner * width + index - start < limit
    return req, patch, live


def split_index(shape, dim, size, count):
    index = lax.broadcasted_iota(jnp.int32, shape, dim)
    owner = jnp.zeros_like(index)
    for j in range(1, count):
        owner = owner + jnp.where(index >= j * size, 1, 0)
    return owner, index - owner * size


def kernel(dims, lengths_ref, text_len_ref, act_ref, video_ref, text_ref, stale_ref, w_mod_hbm,
           w_qkv_hbm, w_out_hbm, hidden_video, hidden_text, cache_video, cache_text,
           w_mod, w_qkv, w_out, x_buf, normed, projected, attended, result, mod_all, heads_send, heads_recv,
           back_send, back_recv, stale_send_buf, stale_recv_buf, key_cat, value_cat, part_send, part_recv, bias,
           w_sem, mod_send, mod_recv, stale_send, stale_recv, heads_out, heads_in, back_out, back_in, p_send, p_recv,
           cross_send, cross_recv, x_send, x_recv, res_send, res_recv):
    requests, patches, per_dev, text_dev, n_seq, n_mp, width, cols = dims
    rows = requests * (patches * per_dev + text_dev)
    video_rows = requests * patches * per_dev
    stale_rows = requests * (patches - 1) * per_dev
    groups = cols // GROUP
    each, active = head_split(cols // HEAD, n_seq)
    share = each * HEAD
    fresh_keys = n_seq * rows
    section = lax.axis_index("section")
    seq = lax.axis_index("seq")
    mp = lax.axis_index("mp")
    other = 1 - section
    core_mate = mp + 1 - 2 * lax.rem(mp, 2)
    y_mate = lax.rem(mp + 2, n_mp)
    diagonal = lax.rem(core_mate + 2, n_mp)
    half = rows // 32 * 16 + 16 * (rows // 16 % 2)
    row_pieces = (pl.ds(0, half), pl.ds(half, rows - half))
    row_slices = (slice(0, half), slice(half, rows))

    def at(sec, se, m):
        return (sec, se, m)

    mod_pieces = 4
    mod_piece = w_mod.shape[0] // mod_pieces
    mod_weights = [
        pltpu.make_async_copy(w_mod_hbm.at[pl.ds(i * mod_piece, mod_piece)], w_mod.at[pl.ds(i * mod_piece, mod_piece)],
                              w_sem.at[11 + i]) for i in range(mod_pieces)]
    for copy in mod_weights:
        copy.start()
    weight_copies = []
    pieces = 3
    piece = width // pieces
    for part in (1, 2, 0):
        for i in range(pieces):
            weight_copies.append(pltpu.make_async_copy(
                w_qkv_hbm.at[part, pl.ds(i * piece, piece)],
                w_qkv.at[part, pl.ds(i * piece, piece)],
                w_sem.at[1 + part * pieces + i]))
    weight_copies.append(pltpu.make_async_copy(w_out_hbm, w_out, w_sem.at[1 + 3 * pieces]))
    barrier = pltpu.get_barrier_semaphore()
    for k in range(1, n_mp):
        pl.semaphore_signal(barrier, inc=1, device_id=at(section, seq, lax.rem(mp + k, n_mp)), device_id_type=MESH)
    for k in range(1, n_seq):
        pl.semaphore_signal(barrier, inc=1, device_id=at(section, lax.rem(seq + k, n_seq), mp), device_id_type=MESH)
    pl.semaphore_signal(barrier, inc=1, device_id=at(other, seq, mp), device_id_type=MESH)

    for copy in mod_weights:
        copy.wait()
    for copy in weight_copies:
        copy.start()
    act = jnp.broadcast_to(act_ref[...].astype(F32), (8, act_ref.shape[1])).astype(BF16)
    mod_all[mp] = jnp.dot(act, w_mod[...], preferred_element_type=F32)
    pl.semaphore_wait(barrier, n_mp - 1 + n_seq - 1 + 1)

    def mod_copy(k):
        return pltpu.make_async_remote_copy(
            src_ref=mod_all.at[mp], dst_ref=mod_all.at[mp], send_sem=mod_send.at[k],
            recv_sem=mod_recv.at[k], device_id=at(section, seq, lax.rem(mp + k, n_mp)), device_id_type=MESH)

    def mod_arrival(k):
        origin = lax.rem(mp + n_mp - k, n_mp)
        return pltpu.make_async_remote_copy(
            src_ref=mod_all.at[origin], dst_ref=mod_all.at[origin], send_sem=mod_send.at[k],
            recv_sem=mod_recv.at[k], device_id=at(section, seq, origin), device_id_type=MESH)

    def to_device(send, recv, sems, d):
        return pltpu.make_async_remote_copy(
            src_ref=send.at[d], dst_ref=recv.at[seq], send_sem=sems[0].at[d], recv_sem=sems[1].at[seq],
            device_id=at(section, d, mp), device_id_type=MESH)

    def from_device(send, recv, sems, origin):
        return pltpu.make_async_remote_copy(
            src_ref=recv.at[origin], dst_ref=recv.at[origin], send_sem=sems[0].at[origin], recv_sem=sems[1].at[origin],
            device_id=at(section, origin, mp), device_id_type=MESH)

    def send_part(exchange, d):
        @pl.when(seq != d)
        def _():
            to_device(*exchange, d).start()

    def keep_part(exchange, d):
        @pl.when(seq == d)
        def _():
            exchange[1][d] = exchange[0][d]

    def sent_part(exchange, d):
        @pl.when(seq != d)
        def _():
            to_device(*exchange, d).wait_send()

    stale_exchange = (stale_send_buf, stale_recv_buf, (stale_send, stale_recv))
    heads_exchange = (heads_send, heads_recv, (heads_out, heads_in))
    back_exchange = (back_send, back_recv, (back_out, back_in))

    def when_active(function):
        if active == n_seq:
            function()
        else:
            pl.when(seq < active)(function)

    for k in range(1, n_mp):
        mod_copy(k).start()

    span_all = patches * per_dev
    for kind in range(2):
        whole = stale_ref[:, kind, :].astype(F32)
        kept = jnp.concatenate(
            [whole[r * span_all + per_dev:(r + 1) * span_all] for r in range(requests)], axis=0).astype(BF16)
        for d in range(active):
            stale_send_buf[d, :, kind * share:(kind + 1) * share] = kept[:, d * share:(d + 1) * share]
    for d in range(active):
        send_part(stale_exchange, d)
        keep_part(stale_exchange, d)

    row_index = lax.broadcasted_iota(jnp.int32, (rows, 1), 0)
    row_req, row_patch, _ = slot_marks(
        row_index, lengths_ref, text_len_ref, requests, 0, patches, per_dev, text_dev, 0)
    key_owner, key_index = split_index((1, n_seq * rows), 1, rows, n_seq)
    key_req, key_patch, key_live = slot_marks(
        key_index, lengths_ref, text_len_ref, requests, 0, patches, per_dev, text_dev, key_owner)
    key_limit = jnp.where(key_live, key_patch, patches)
    bias[:, :fresh_keys] = jnp.where((row_req == key_req) & (key_limit <= row_patch), 0.0, NEG)
    key_owner, key_index = split_index((1, n_seq * stale_rows), 1, stale_rows, n_seq)
    key_req, key_patch, key_live = slot_marks(
        key_index, lengths_ref, text_len_ref, requests, 1, patches, per_dev, 0, key_owner)
    key_limit = jnp.where(key_live, key_patch, -1)
    bias[:, fresh_keys:] = jnp.where((row_req == key_req) & (key_limit > row_patch), 0.0, NEG)

    @pl.when(section == 0)
    def _():
        x_buf[pl.ds(0, video_rows)] = video_ref[...]
        x_buf[pl.ds(video_rows, rows - video_rows)] = text_ref[...]

    def block(j):
        return pl.ds(pl.multiple_of(j * cols, SLAB), cols)

    def cross_copy(c):
        return pltpu.make_async_remote_copy(
            src_ref=result.at[row_pieces[c], block(mp)], dst_ref=x_buf.at[row_pieces[c], block(mp)],
            send_sem=cross_send.at[c], recv_sem=cross_recv.at[c], device_id=at(other, seq, mp), device_id_type=MESH)

    def spread_copy(buffer, sems, c, kind, origin):
        part = buffer.at[row_pieces[c], block(origin)]
        return pltpu.make_async_remote_copy(
            src_ref=part, dst_ref=part, send_sem=sems[0].at[c, kind], recv_sem=sems[1].at[c, kind],
            device_id=at(section, seq, y_mate if kind == 1 else core_mate), device_id_type=MESH)

    def spread_start(buffer, sems, c):
        spread_copy(buffer, sems, c, 1, mp).start()
        spread_copy(buffer, sems, c, 0, mp).start()

    def spread_finish(buffer, sems):
        for c in range(2):
            spread_copy(buffer, sems, c, 1, y_mate).wait_recv()
            spread_copy(buffer, sems, c, 2, y_mate).start()
        for c in range(2):
            spread_copy(buffer, sems, c, 0, core_mate).wait_recv()
            spread_copy(buffer, sems, c, 2, diagonal).wait_recv()

    def spread_sent(buffer, sems):
        for c in range(2):
            for kind, origin in enumerate((mp, mp, y_mate)):
                spread_copy(buffer, sems, c, kind, origin).wait_send()

    x_sems, result_sems = (x_send, x_recv), (res_send, res_recv)

    @pl.when(section == 1)
    def _():
        for c in range(2):
            cross_copy(c).wait_recv()
            spread_start(x_buf, x_sems, c)
        spread_finish(x_buf, x_sems)

    def modulated(b):
        return mod_all[b // 3, 0:1, (b % 3) * cols:(b % 3 + 1) * cols]

    values = x_buf[...].astype(F32)
    mean = jnp.mean(values, axis=-1, keepdims=True)
    center = values - mean
    inverse = lax.rsqrt(jnp.mean(center * center, axis=-1, keepdims=True) + EPS)
    for k in range(1, n_mp):
        mod_arrival(k).wait_recv()
    for c in range(n_mp):
        span = slice(c * cols, (c + 1) * cols)
        piece_values = (x_buf[:, span].astype(F32) - mean) * inverse
        normed[:, span] = (piece_values * (1.0 + modulated(n_mp + c)) + modulated(c)).astype(BF16)

    def project(part, g):
        return jnp.dot(normed[...], w_qkv[part, :, g * GROUP:(g + 1) * GROUP], preferred_element_type=F32)

    middle = (n_seq + 1) // 2
    lower = 1 - seq // middle

    def project_all(order):
        done, sent = set(), set()
        for g in order:
            for index, part in enumerate((1, 2, 0)):
                if g == order[0]:
                    for copy in weight_copies[index * pieces:(index + 1) * pieces]:
                        copy.wait()
                tile = project(part, g).astype(BF16)
                if part == 0:
                    tile = (tile.astype(F32) * HEAD ** (-0.5)).astype(BF16)
                projected[part, :, g * GROUP:(g + 1) * GROUP] = tile
            done.add(g)
            for d in sorted(range(active), reverse=order[0] != 0):
                first, last = d * share // GROUP, ((d + 1) * share - 1) // GROUP
                if d not in sent and all(t in done for t in range(first, last + 1)):
                    sent.add(d)
                    for part in range(3):
                        heads_send[d, :, part * share:(part + 1) * share] = (
                            projected[part, :, d * share:(d + 1) * share])
                    send_part(heads_exchange, d)
                    keep_part(heads_exchange, d)

    @pl.when(lower == 1)
    def _():
        project_all(tuple(reversed(range(groups))))

    @pl.when(lower == 0)
    def _():
        project_all(tuple(range(groups)))

    for g in range(groups):
        for kind in range(2):
            span = slice(g * GROUP, (g + 1) * GROUP)
            part = projected[1 + kind, :, span]
            cache_video[:, kind, span] = part[:video_rows]
            cache_text[:, kind, span] = part[video_rows:]

    @when_active
    def _():
        for k in range(1, n_seq):
            from_device(*stale_exchange, lax.rem(seq + n_seq - k, n_seq)).wait_recv()
        for h in range(each):
            for kind, cat in enumerate((key_cat, value_cat)):
                at_col = kind * share + h * HEAD
                cat[h, fresh_keys:] = stale_recv_buf[:, :, at_col:at_col + HEAD].reshape(n_seq * stale_rows, HEAD)
        for k in range(1, n_seq):
            from_device(*heads_exchange, lax.rem(seq + n_seq - k, n_seq)).wait_recv()
        for h in range(each):
            for kind, cat in enumerate((key_cat, value_cat)):
                at_col = (1 + kind) * share + h * HEAD
                cat[h, :fresh_keys] = heads_recv[:, :, at_col:at_col + HEAD].reshape(fresh_keys, HEAD)
        for i in range(n_seq):
            d = i + lower * (n_seq - 1 - 2 * i)
            for h in range(each):
                heads_at = slice(h * HEAD, (h + 1) * HEAD)
                scores = lax.dot_general(
                    heads_recv[d, :, heads_at], key_cat[h], (((1,), (1,)), ((), ())), preferred_element_type=F32)
                scores = scores + bias[...]
                top = jnp.max(scores, axis=-1, keepdims=True)
                weights = jnp.exp(scores - top)
                total = jnp.sum(weights, axis=-1, keepdims=True)
                mixed = jnp.dot(weights.astype(BF16), value_cat[h], preferred_element_type=F32)
                back_send[d, :, heads_at] = (mixed / total).astype(BF16)
            send_part(back_exchange, d)
            keep_part(back_exchange, d)

    for d in range(active):
        @pl.when(seq != d)
        def _():
            from_device(*back_exchange, d).wait_recv()
    for d in range(active):
        attended[:, d * share:(d + 1) * share] = back_recv[d, :, :share]

    def part_copy(k):
        return pltpu.make_async_remote_copy(
            src_ref=part_send.at[k], dst_ref=part_recv.at[k], send_sem=p_send.at[k], recv_sem=p_recv.at[k],
            device_id=at(section, seq, core_mate), device_id_type=MESH)

    def y_copy(c):
        return pltpu.make_async_remote_copy(
            src_ref=part_send.at[2, row_pieces[c]], dst_ref=part_recv.at[2, row_pieces[c]],
            send_sem=p_send.at[2 + c], recv_sem=p_recv.at[2 + c],
            device_id=at(section, seq, y_mate), device_id_type=MESH)

    weight_copies[-1].wait()

    def out_block(j):
        return jnp.dot(attended[...], w_out[:, block(j)], preferred_element_type=F32)

    part_send[0] = out_block(diagonal).astype(BF16)
    part_copy(0).start()
    passed = out_block(y_mate)
    part_copy(0).wait_recv()
    for c in range(2):
        at_rows = row_slices[c]
        part_send[2, at_rows] = (passed[at_rows] + part_recv[0, at_rows].astype(F32)).astype(BF16)
        y_copy(c).start()
    part_send[1] = out_block(core_mate).astype(BF16)
    part_copy(1).start()
    summed = out_block(mp)
    part_copy(1).wait_recv()
    summed = summed + part_recv[1].astype(F32)
    gate_at = 2 * n_mp + mp
    gate = mod_all[gate_at // 3, 0:1, pl.ds(pl.multiple_of(gate_at % 3 * cols, SLAB), cols)]
    for c in range(2):
        at_rows = row_slices[c]
        y_copy(c).wait_recv()
        whole_sum = summed[at_rows] + part_recv[2, at_rows].astype(F32)
        result[at_rows, block(mp)] = (x_buf[at_rows, block(mp)].astype(F32) + gate * whole_sum).astype(BF16)

        @pl.when(section == 0)
        def _():
            cross_copy(c).start()

        spread_start(result, result_sems, c)
    spread_finish(result, result_sems)
    hidden_video[...] = result[pl.ds(0, video_rows)]
    hidden_text[...] = result[pl.ds(video_rows, rows - video_rows)]

    @pl.when(section == 0)
    def _():
        for c in range(2):
            cross_copy(c).wait_send()

    @pl.when(section == 1)
    def _():
        spread_sent(x_buf, x_sems)

    spread_sent(result, result_sems)
    for k in range(1, n_mp):
        mod_copy(k).wait_send()
    for k in range(2):
        part_copy(k).wait_send()
        y_copy(k).wait_send()
    for d in range(active):
        sent_part(stale_exchange, d)
        sent_part(heads_exchange, d)

    @when_active
    def _():
        for d in range(n_seq):
            sent_part(back_exchange, d)


def store_kernel(*refs):
    ins, outs, held, sems = refs[:4], refs[4:8], refs[8:12], refs[12]
    loads = [pltpu.make_async_copy(ins[i], held[i], sems.at[0, i]) for i in range(4)]
    stores = [pltpu.make_async_copy(held[i], outs[i], sems.at[1, i]) for i in range(4)]
    for copy in loads:
        copy.start()
    for load, store in zip(loads, stores):
        load.wait()
        store.start()
    for copy in stores:
        copy.wait()


def padded(count):
    return -(-count // SLAB) * SLAB


def head_split(heads, n_seq):
    each = -(-heads // n_seq)
    while heads % each:
        each += 1
    return each, heads // each


def body(video, text, patch_lengths, text_len, timestep, w_mod, w_qkv, w_out, stale_cache):
    n_seq, n_mp = lax.axis_size("seq"), lax.axis_size("mp")
    requests, patches, per_dev, width = video.shape
    text_dev = text.shape[1]
    cols = w_out.shape[1]
    each, active = head_split(cols // HEAD, n_seq)
    share = each * HEAD
    rows = requests * (patches * per_dev + text_dev)
    video_rows = requests * patches * per_dev
    text_rows = requests * text_dev
    stale_rows = requests * (patches - 1) * per_dev

    half_width = w_mod.shape[1] // 2
    frequency = jnp.exp(-math.log(10000.0) * jnp.arange(half_width, dtype=F32) / half_width)
    phases = timestep.astype(F32)[0] * frequency
    embedding = jnp.concatenate([jnp.cos(phases), jnp.sin(phases)])
    act = jax.nn.silu(embedding).astype(BF16)

    mod_cols = w_mod.shape[2]
    keys = n_seq * (rows + stale_rows)
    dims = (requests, patches, per_dev, text_dev, n_seq, n_mp, width, cols)
    vmem = pl.BlockSpec(memory_space=pltpu.VMEM)
    smem = pl.BlockSpec(memory_space=pltpu.SMEM)
    hbm = pl.BlockSpec(memory_space=pl.ANY)
    dma = pltpu.SemaphoreType.DMA
    outputs = pl.pallas_call(
        functools.partial(kernel, dims),
        out_shape=(
            jax.ShapeDtypeStruct((video_rows, width), BF16),
            jax.ShapeDtypeStruct((text_rows, width), BF16),
            jax.ShapeDtypeStruct((video_rows, 2, cols), BF16),
            jax.ShapeDtypeStruct((text_rows, 2, cols), BF16),
        ),
        in_specs=[smem, smem, vmem, vmem, vmem, vmem, hbm, hbm, hbm],
        out_specs=(vmem,) * 4,
        scratch_shapes=[
            pltpu.VMEM(w_mod.shape[1:], BF16),
            pltpu.VMEM((3, width, cols), BF16),
            pltpu.VMEM((cols, width), BF16),
            pltpu.VMEM((rows, width), BF16),
            pltpu.VMEM((rows, width), BF16),
            pltpu.VMEM((3, rows, cols), BF16),
            pltpu.VMEM((rows, cols), BF16),
            pltpu.VMEM((rows, width), BF16),
            pltpu.VMEM((n_mp, 8, mod_cols), F32),
            pltpu.VMEM((active, rows, padded(3 * share)), BF16),
            pltpu.VMEM((n_seq, rows, padded(3 * share)), BF16),
            pltpu.VMEM((n_seq, rows, padded(share)), BF16),
            pltpu.VMEM((n_seq, rows, padded(share)), BF16),
            pltpu.VMEM((active, stale_rows, padded(2 * share)), BF16),
            pltpu.VMEM((n_seq, stale_rows, padded(2 * share)), BF16),
            pltpu.VMEM((each, keys, HEAD), BF16),
            pltpu.VMEM((each, keys, HEAD), BF16),
            pltpu.VMEM((3, rows, cols), BF16),
            pltpu.VMEM((3, rows, cols), BF16),
            pltpu.VMEM((rows, keys), F32),
            dma((15,)),
            dma((n_mp,)), dma((n_mp,)),
            dma((n_seq,)), dma((n_seq,)),
            dma((n_seq,)), dma((n_seq,)),
            dma((n_seq,)), dma((n_seq,)),
            dma((4,)), dma((4,)),
            dma((2,)), dma((2,)),
            dma((2, 3)), dma((2, 3)),
            dma((2, 3)), dma((2, 3)),
        ],
        compiler_params=pltpu.CompilerParams(
            collective_id=0, has_side_effects=True, vmem_limit_bytes=56 * 1024 * 1024
        ),
        cost_estimate=pl.CostEstimate(
            flops=2 * rows * width * 4 * cols, bytes_accessed=2 * width * (4 * cols + 2 * half_width), transcendentals=0
        ),
        name="layer",
    )(
        patch_lengths, text_len, act[None, :],
        video.reshape(video_rows, width), text.reshape(text_rows, width), stale_cache.reshape(video_rows, 2, cols),
        w_mod[0], w_qkv[0].transpose(1, 0, 2), w_out[0],
    )
    hidden_video, hidden_text, cache_video, cache_text = pl.pallas_call(
        store_kernel,
        out_shape=tuple(jax.ShapeDtypeStruct(o.shape, o.dtype) for o in outputs),
        in_specs=[hbm] * 4,
        out_specs=(hbm,) * 4,
        scratch_shapes=[pltpu.VMEM(o.shape, o.dtype) for o in outputs] + [dma((2, 4))],
        compiler_params=pltpu.CompilerParams(vmem_limit_bytes=56 * 1024 * 1024),
        name="store",
    )(*outputs)
    return (
        hidden_video.reshape(1, requests, patches, per_dev, width),
        hidden_text.reshape(1, requests, text_dev, width),
        cache_video.reshape(1, requests, patches, per_dev, 2, cols),
        cache_text.reshape(1, requests, text_dev, 2, cols),
    )


def solution(mesh):
    placed = (
        P(None, None, "seq", None),
        P(None, "seq", None),
        P(),
        P(),
        P(),
        P("section", None, "mp"),
        P("section", None, None, "mp"),
        P("section", "mp", None),
        P("section", None, None, "seq", None, "mp"),
    )
    return jax.shard_map(
        body,
        mesh=mesh,
        in_specs=placed,
        out_specs=(
            P("section", None, None, "seq", None),
            P("section", None, "seq", None),
            P("section", None, None, "seq", None, "mp"),
            P("section", None, "seq", None, "mp"),
        ),
        check_vma=False,
    )
```

```python
import functools
import math

import jax
import jax.numpy as jnp
from jax import lax
from jax.experimental import pallas as pl
from jax.experimental.pallas import tpu as pltpu
from jax.sharding import PartitionSpec as P

HEAD = 64
EPS = 1e-05
NEG = -1e30
SLAB = 128
GROUP = 256
MESH = pl.DeviceIdType.MESH
F32 = jnp.float32
BF16 = jnp.bfloat16


def slot_marks(index, lengths_ref, text_ref, requests, first, patches, per_dev, text_dev, owner):
    req = jnp.zeros_like(index)
    patch = jnp.zeros_like(index)
    limit = jnp.zeros_like(index)
    start = jnp.zeros_like(index)
    at = 0
    for r in range(requests):
        for p in range(first, patches):
            inside = (index >= at) & (index < at + per_dev)
            req = jnp.where(inside, r, req)
            patch = jnp.where(inside, p, patch)
            limit = jnp.where(inside, lengths_ref[r, p], limit)
            start = jnp.where(inside, at, start)
            at += per_dev
    width = jnp.full_like(index, per_dev)
    for r in range(requests if text_dev else 0):
        inside = (index >= at) & (index < at + text_dev)
        req = jnp.where(inside, r, req)
        limit = jnp.where(inside, text_ref[r], limit)
        start = jnp.where(inside, at, start)
        width = jnp.where(inside, text_dev, width)
        at += text_dev
    live = owner * width + index - start < limit
    return req, patch, live


def split_index(shape, dim, size, count):
    index = lax.broadcasted_iota(jnp.int32, shape, dim)
    owner = jnp.zeros_like(index)
    for j in range(1, count):
        owner = owner + jnp.where(index >= j * size, 1, 0)
    return owner, index - owner * size


def kernel(dims, lengths_ref, text_len_ref, act_ref, video_ref, text_ref, stale_ref, w_mod_hbm,
           w_qkv_hbm, w_out_hbm, hidden_video, hidden_text, cache_video, cache_text,
           w_mod, w_qkv, w_out, x_buf, normed, projected, attended, result, mod_all, heads_send, heads_recv,
           back_send, back_recv, stale_held, cache_held, stale_send_buf, stale_recv_buf, key_cat, value_cat, part_send, part_recv, bias,
           w_sem, mod_send, mod_recv, stale_send, stale_recv, heads_out, heads_in, back_out, back_in, p_send, p_recv,
           cross_send, cross_recv, x_send, x_recv, res_send, res_recv, in_sem, out_sem):
    requests, patches, per_dev, text_dev, n_seq, n_mp, width, cols = dims
    rows = requests * (patches * per_dev + text_dev)
    video_rows = requests * patches * per_dev
    stale_rows = requests * (patches - 1) * per_dev
    groups = cols // GROUP
    each, active = head_split(cols // HEAD, n_seq)
    share = each * HEAD
    fresh_keys = n_seq * rows
    section = lax.axis_index("section")
    seq = lax.axis_index("seq")
    mp = lax.axis_index("mp")
    other = 1 - section
    core_mate = mp + 1 - 2 * lax.rem(mp, 2)
    y_mate = lax.rem(mp + 2, n_mp)
    diagonal = lax.rem(core_mate + 2, n_mp)
    half = rows // 32 * 16 + 16 * (rows // 16 % 2)
    row_pieces = (pl.ds(0, half), pl.ds(half, rows - half))
    row_slices = (slice(0, half), slice(half, rows))

    def at(sec, se, m):
        return (sec, se, m)

    mod_pieces = 4
    mod_piece = w_mod.shape[0] // mod_pieces
    mod_weights = [
        pltpu.make_async_copy(w_mod_hbm.at[pl.ds(i * mod_piece, mod_piece)], w_mod.at[pl.ds(i * mod_piece, mod_piece)],
                              w_sem.at[11 + i]) for i in range(mod_pieces)]
    for copy in mod_weights:
        copy.start()
    in_copies = [
        pltpu.make_async_copy(video_ref, x_buf.at[pl.ds(0, video_rows)], in_sem.at[0]),
        pltpu.make_async_copy(text_ref, x_buf.at[pl.ds(video_rows, rows - video_rows)], in_sem.at[1]),
        pltpu.make_async_copy(stale_ref, stale_held, in_sem.at[2])]
    out_copies = [
        pltpu.make_async_copy(result.at[pl.ds(0, video_rows)], hidden_video, out_sem.at[0]),
        pltpu.make_async_copy(result.at[pl.ds(video_rows, rows - video_rows)], hidden_text, out_sem.at[1]),
        pltpu.make_async_copy(cache_held.at[pl.ds(0, video_rows)], cache_video, out_sem.at[2]),
        pltpu.make_async_copy(cache_held.at[pl.ds(video_rows, rows - video_rows)], cache_text, out_sem.at[3])]
    in_copies[2].start()

    @pl.when(section == 0)
    def _():
        in_copies[0].start()
        in_copies[1].start()

    weight_copies = []
    pieces = 3
    piece = width // pieces
    for part in (1, 2, 0):
        for i in range(pieces):
            weight_copies.append(pltpu.make_async_copy(
                w_qkv_hbm.at[part, pl.ds(i * piece, piece)],
                w_qkv.at[part, pl.ds(i * piece, piece)],
                w_sem.at[1 + part * pieces + i]))
    weight_copies.append(pltpu.make_async_copy(w_out_hbm, w_out, w_sem.at[1 + 3 * pieces]))
    barrier = pltpu.get_barrier_semaphore()
    for k in range(1, n_mp):
        pl.semaphore_signal(barrier, inc=1, device_id=at(section, seq, lax.rem(mp + k, n_mp)), device_id_type=MESH)
    for k in range(1, n_seq):
        pl.semaphore_signal(barrier, inc=1, device_id=at(section, lax.rem(seq + k, n_seq), mp), device_id_type=MESH)
    pl.semaphore_signal(barrier, inc=1, device_id=at(other, seq, mp), device_id_type=MESH)

    for copy in mod_weights:
        copy.wait()
    for copy in weight_copies:
        copy.start()
    act = jnp.broadcast_to(act_ref[...].astype(F32), (8, act_ref.shape[1])).astype(BF16)
    mod_all[mp] = jnp.dot(act, w_mod[...], preferred_element_type=F32)
    pl.semaphore_wait(barrier, n_mp - 1 + n_seq - 1 + 1)

    def mod_copy(k):
        return pltpu.make_async_remote_copy(
            src_ref=mod_all.at[mp], dst_ref=mod_all.at[mp], send_sem=mod_send.at[k],
            recv_sem=mod_recv.at[k], device_id=at(section, seq, lax.rem(mp + k, n_mp)), device_id_type=MESH)

    def mod_arrival(k):
        origin = lax.rem(mp + n_mp - k, n_mp)
        return pltpu.make_async_remote_copy(
            src_ref=mod_all.at[origin], dst_ref=mod_all.at[origin], send_sem=mod_send.at[k],
            recv_sem=mod_recv.at[k], device_id=at(section, seq, origin), device_id_type=MESH)

    def to_device(send, recv, sems, d):
        return pltpu.make_async_remote_copy(
            src_ref=send.at[d], dst_ref=recv.at[seq], send_sem=sems[0].at[d], recv_sem=sems[1].at[seq],
            device_id=at(section, d, mp), device_id_type=MESH)

    def from_device(send, recv, sems, origin):
        return pltpu.make_async_remote_copy(
            src_ref=recv.at[origin], dst_ref=recv.at[origin], send_sem=sems[0].at[origin], recv_sem=sems[1].at[origin],
            device_id=at(section, origin, mp), device_id_type=MESH)

    def send_part(exchange, d):
        @pl.when(seq != d)
        def _():
            to_device(*exchange, d).start()

    def keep_part(exchange, d):
        @pl.when(seq == d)
        def _():
            exchange[1][d] = exchange[0][d]

    def sent_part(exchange, d):
        @pl.when(seq != d)
        def _():
            to_device(*exchange, d).wait_send()

    stale_exchange = (stale_send_buf, stale_recv_buf, (stale_send, stale_recv))
    heads_exchange = (heads_send, heads_recv, (heads_out, heads_in))
    back_exchange = (back_send, back_recv, (back_out, back_in))

    def when_active(function):
        if active == n_seq:
            function()
        else:
            pl.when(seq < active)(function)

    for k in range(1, n_mp):
        mod_copy(k).start()

    span_all = patches * per_dev
    in_copies[2].wait()
    for kind in range(2):
        whole = stale_held[:, kind, :].astype(F32)
        kept = jnp.concatenate(
            [whole[r * span_all + per_dev:(r + 1) * span_all] for r in range(requests)], axis=0).astype(BF16)
        for d in range(active):
            stale_send_buf[d, :, kind * share:(kind + 1) * share] = kept[:, d * share:(d + 1) * share]
    for d in range(active):
        send_part(stale_exchange, d)
        keep_part(stale_exchange, d)

    row_index = lax.broadcasted_iota(jnp.int32, (rows, 1), 0)
    row_req, row_patch, _ = slot_marks(
        row_index, lengths_ref, text_len_ref, requests, 0, patches, per_dev, text_dev, 0)
    key_owner, key_index = split_index((1, n_seq * rows), 1, rows, n_seq)
    key_req, key_patch, key_live = slot_marks(
        key_index, lengths_ref, text_len_ref, requests, 0, patches, per_dev, text_dev, key_owner)
    key_limit = jnp.where(key_live, key_patch, patches)
    bias[:, :fresh_keys] = jnp.where((row_req == key_req) & (key_limit <= row_patch), 0.0, NEG)
    key_owner, key_index = split_index((1, n_seq * stale_rows), 1, stale_rows, n_seq)
    key_req, key_patch, key_live = slot_marks(
        key_index, lengths_ref, text_len_ref, requests, 1, patches, per_dev, 0, key_owner)
    key_limit = jnp.where(key_live, key_patch, -1)
    bias[:, fresh_keys:] = jnp.where((row_req == key_req) & (key_limit > row_patch), 0.0, NEG)

    @pl.when(section == 0)
    def _():
        in_copies[0].wait()
        in_copies[1].wait()

    def block(j):
        return pl.ds(pl.multiple_of(j * cols, SLAB), cols)

    def cross_copy(c):
        return pltpu.make_async_remote_copy(
            src_ref=result.at[row_pieces[c], block(mp)], dst_ref=x_buf.at[row_pieces[c], block(mp)],
            send_sem=cross_send.at[c], recv_sem=cross_recv.at[c], device_id=at(other, seq, mp), device_id_type=MESH)

    def spread_copy(buffer, sems, c, kind, origin):
        part = buffer.at[row_pieces[c], block(origin)]
        return pltpu.make_async_remote_copy(
            src_ref=part, dst_ref=part, send_sem=sems[0].at[c, kind], recv_sem=sems[1].at[c, kind],
            device_id=at(section, seq, y_mate if kind == 1 else core_mate), device_id_type=MESH)

    def spread_start(buffer, sems, c):
        spread_copy(buffer, sems, c, 1, mp).start()
        spread_copy(buffer, sems, c, 0, mp).start()

    def spread_finish(buffer, sems):
        for c in range(2):
            spread_copy(buffer, sems, c, 1, y_mate).wait_recv()
            spread_copy(buffer, sems, c, 2, y_mate).start()
        for c in range(2):
            spread_copy(buffer, sems, c, 0, core_mate).wait_recv()
            spread_copy(buffer, sems, c, 2, diagonal).wait_recv()

    def spread_sent(buffer, sems):
        for c in range(2):
            for kind, origin in enumerate((mp, mp, y_mate)):
                spread_copy(buffer, sems, c, kind, origin).wait_send()

    x_sems, result_sems = (x_send, x_recv), (res_send, res_recv)

    @pl.when(section == 1)
    def _():
        for c in range(2):
            cross_copy(c).wait_recv()
            spread_start(x_buf, x_sems, c)
        spread_finish(x_buf, x_sems)

    def modulated(b):
        return mod_all[b // 3, 0:1, (b % 3) * cols:(b % 3 + 1) * cols]

    values = x_buf[...].astype(F32)
    mean = jnp.mean(values, axis=-1, keepdims=True)
    center = values - mean
    inverse = lax.rsqrt(jnp.mean(center * center, axis=-1, keepdims=True) + EPS)
    for k in range(1, n_mp):
        mod_arrival(k).wait_recv()
    for c in range(n_mp):
        span = slice(c * cols, (c + 1) * cols)
        piece_values = (x_buf[:, span].astype(F32) - mean) * inverse
        normed[:, span] = (piece_values * (1.0 + modulated(n_mp + c)) + modulated(c)).astype(BF16)

    def project(part, g):
        return jnp.dot(normed[...], w_qkv[part, :, g * GROUP:(g + 1) * GROUP], preferred_element_type=F32)

    middle = (n_seq + 1) // 2
    lower = 1 - seq // middle

    def project_all(order):
        done, sent = set(), set()
        for g in order:
            for index, part in enumerate((1, 2, 0)):
                if g == order[0]:
                    for copy in weight_copies[index * pieces:(index + 1) * pieces]:
                        copy.wait()
                tile = project(part, g).astype(BF16)
                if part == 0:
                    tile = (tile.astype(F32) * HEAD ** (-0.5)).astype(BF16)
                projected[part, :, g * GROUP:(g + 1) * GROUP] = tile
            done.add(g)
            for d in sorted(range(active), reverse=order[0] != 0):
                first, last = d * share // GROUP, ((d + 1) * share - 1) // GROUP
                if d not in sent and all(t in done for t in range(first, last + 1)):
                    sent.add(d)
                    for part in range(3):
                        heads_send[d, :, part * share:(part + 1) * share] = (
                            projected[part, :, d * share:(d + 1) * share])
                    send_part(heads_exchange, d)
                    keep_part(heads_exchange, d)

    @pl.when(lower == 1)
    def _():
        project_all(tuple(reversed(range(groups))))

    @pl.when(lower == 0)
    def _():
        project_all(tuple(range(groups)))

    for g in range(groups):
        for kind in range(2):
            span = slice(g * GROUP, (g + 1) * GROUP)
            cache_held[:, kind, span] = projected[1 + kind, :, span]
    out_copies[2].start()
    out_copies[3].start()

    @when_active
    def _():
        for k in range(1, n_seq):
            from_device(*stale_exchange, lax.rem(seq + n_seq - k, n_seq)).wait_recv()
        for h in range(each):
            for kind, cat in enumerate((key_cat, value_cat)):
                at_col = kind * share + h * HEAD
                cat[h, fresh_keys:] = stale_recv_buf[:, :, at_col:at_col + HEAD].reshape(n_seq * stale_rows, HEAD)
        for k in range(1, n_seq):
            from_device(*heads_exchange, lax.rem(seq + n_seq - k, n_seq)).wait_recv()
        for h in range(each):
            for kind, cat in enumerate((key_cat, value_cat)):
                at_col = (1 + kind) * share + h * HEAD
                cat[h, :fresh_keys] = heads_recv[:, :, at_col:at_col + HEAD].reshape(fresh_keys, HEAD)
        for i in range(n_seq):
            d = i + lower * (n_seq - 1 - 2 * i)
            for h in range(each):
                heads_at = slice(h * HEAD, (h + 1) * HEAD)
                scores = lax.dot_general(
                    heads_recv[d, :, heads_at], key_cat[h], (((1,), (1,)), ((), ())), preferred_element_type=F32)
                scores = scores + bias[...]
                top = jnp.max(scores, axis=-1, keepdims=True)
                weights = jnp.exp(scores - top)
                total = jnp.sum(weights, axis=-1, keepdims=True)
                mixed = jnp.dot(weights.astype(BF16), value_cat[h], preferred_element_type=F32)
                back_send[d, :, heads_at] = (mixed / total).astype(BF16)
            send_part(back_exchange, d)
            keep_part(back_exchange, d)

    for d in range(active):
        @pl.when(seq != d)
        def _():
            from_device(*back_exchange, d).wait_recv()
    for d in range(active):
        attended[:, d * share:(d + 1) * share] = back_recv[d, :, :share]

    def part_copy(k):
        return pltpu.make_async_remote_copy(
            src_ref=part_send.at[k], dst_ref=part_recv.at[k], send_sem=p_send.at[k], recv_sem=p_recv.at[k],
            device_id=at(section, seq, core_mate), device_id_type=MESH)

    def y_copy(c):
        return pltpu.make_async_remote_copy(
            src_ref=part_send.at[2, row_pieces[c]], dst_ref=part_recv.at[2, row_pieces[c]],
            send_sem=p_send.at[2 + c], recv_sem=p_recv.at[2 + c],
            device_id=at(section, seq, y_mate), device_id_type=MESH)

    weight_copies[-1].wait()

    def out_block(j):
        return jnp.dot(attended[...], w_out[:, block(j)], preferred_element_type=F32)

    part_send[0] = out_block(diagonal).astype(BF16)
    part_copy(0).start()
    passed = out_block(y_mate)
    part_copy(0).wait_recv()
    for c in range(2):
        at_rows = row_slices[c]
        part_send[2, at_rows] = (passed[at_rows] + part_recv[0, at_rows].astype(F32)).astype(BF16)
        y_copy(c).start()
    part_send[1] = out_block(core_mate).astype(BF16)
    part_copy(1).start()
    summed = out_block(mp)
    part_copy(1).wait_recv()
    summed = summed + part_recv[1].astype(F32)
    gate_at = 2 * n_mp + mp
    gate = mod_all[gate_at // 3, 0:1, pl.ds(pl.multiple_of(gate_at % 3 * cols, SLAB), cols)]
    for c in range(2):
        at_rows = row_slices[c]
        y_copy(c).wait_recv()
        whole_sum = summed[at_rows] + part_recv[2, at_rows].astype(F32)
        result[at_rows, block(mp)] = (x_buf[at_rows, block(mp)].astype(F32) + gate * whole_sum).astype(BF16)

        @pl.when(section == 0)
        def _():
            cross_copy(c).start()

        spread_start(result, result_sems, c)
    spread_finish(result, result_sems)
    out_copies[0].start()
    out_copies[1].start()

    @pl.when(section == 0)
    def _():
        for c in range(2):
            cross_copy(c).wait_send()

    @pl.when(section == 1)
    def _():
        spread_sent(x_buf, x_sems)

    for copy in out_copies:
        copy.wait()
    spread_sent(result, result_sems)
    for k in range(1, n_mp):
        mod_copy(k).wait_send()
    for k in range(2):
        part_copy(k).wait_send()
        y_copy(k).wait_send()
    for d in range(active):
        sent_part(stale_exchange, d)
        sent_part(heads_exchange, d)

    @when_active
    def _():
        for d in range(n_seq):
            sent_part(back_exchange, d)


def store_kernel(*refs):
    ins, outs, held, sems = refs[:4], refs[4:8], refs[8:12], refs[12]
    loads = [pltpu.make_async_copy(ins[i], held[i], sems.at[0, i]) for i in range(4)]
    stores = [pltpu.make_async_copy(held[i], outs[i], sems.at[1, i]) for i in range(4)]
    for copy in loads:
        copy.start()
    for load, store in zip(loads, stores):
        load.wait()
        store.start()
    for copy in stores:
        copy.wait()


def padded(count):
    return -(-count // SLAB) * SLAB


def head_split(heads, n_seq):
    each = -(-heads // n_seq)
    while heads % each:
        each += 1
    return each, heads // each


def body(video, text, patch_lengths, text_len, timestep, w_mod, w_qkv, w_out, stale_cache):
    n_seq, n_mp = lax.axis_size("seq"), lax.axis_size("mp")
    requests, patches, per_dev, width = video.shape
    text_dev = text.shape[1]
    cols = w_out.shape[1]
    each, active = head_split(cols // HEAD, n_seq)
    share = each * HEAD
    rows = requests * (patches * per_dev + text_dev)
    video_rows = requests * patches * per_dev
    text_rows = requests * text_dev
    stale_rows = requests * (patches - 1) * per_dev

    half_width = w_mod.shape[1] // 2
    frequency = jnp.exp(-math.log(10000.0) * jnp.arange(half_width, dtype=F32) / half_width)
    phases = timestep.astype(F32)[0] * frequency
    embedding = jnp.concatenate([jnp.cos(phases), jnp.sin(phases)])
    act = jax.nn.silu(embedding).astype(BF16)

    mod_cols = w_mod.shape[2]
    keys = n_seq * (rows + stale_rows)
    dims = (requests, patches, per_dev, text_dev, n_seq, n_mp, width, cols)
    vmem = pl.BlockSpec(memory_space=pltpu.VMEM)
    smem = pl.BlockSpec(memory_space=pltpu.SMEM)
    hbm = pl.BlockSpec(memory_space=pl.ANY)
    dma = pltpu.SemaphoreType.DMA
    outputs = pl.pallas_call(
        functools.partial(kernel, dims),
        out_shape=(
            jax.ShapeDtypeStruct((video_rows, width), BF16),
            jax.ShapeDtypeStruct((text_rows, width), BF16),
            jax.ShapeDtypeStruct((video_rows, 2, cols), BF16),
            jax.ShapeDtypeStruct((text_rows, 2, cols), BF16),
        ),
        in_specs=[smem, smem, vmem] + [hbm] * 6,
        out_specs=(hbm,) * 4,
        scratch_shapes=[
            pltpu.VMEM(w_mod.shape[1:], BF16),
            pltpu.VMEM((3, width, cols), BF16),
            pltpu.VMEM((cols, width), BF16),
            pltpu.VMEM((rows, width), BF16),
            pltpu.VMEM((rows, width), BF16),
            pltpu.VMEM((3, rows, cols), BF16),
            pltpu.VMEM((rows, cols), BF16),
            pltpu.VMEM((rows, width), BF16),
            pltpu.VMEM((n_mp, 8, mod_cols), F32),
            pltpu.VMEM((active, rows, padded(3 * share)), BF16),
            pltpu.VMEM((n_seq, rows, padded(3 * share)), BF16),
            pltpu.VMEM((n_seq, rows, padded(share)), BF16),
            pltpu.VMEM((n_seq, rows, padded(share)), BF16),
            pltpu.VMEM((video_rows, 2, cols), BF16),
            pltpu.VMEM((rows, 2, cols), BF16),
            pltpu.VMEM((active, stale_rows, padded(2 * share)), BF16),
            pltpu.VMEM((n_seq, stale_rows, padded(2 * share)), BF16),
            pltpu.VMEM((each, keys, HEAD), BF16),
            pltpu.VMEM((each, keys, HEAD), BF16),
            pltpu.VMEM((3, rows, cols), BF16),
            pltpu.VMEM((3, rows, cols), BF16),
            pltpu.VMEM((rows, keys), F32),
            dma((15,)),
            dma((n_mp,)), dma((n_mp,)),
            dma((n_seq,)), dma((n_seq,)),
            dma((n_seq,)), dma((n_seq,)),
            dma((n_seq,)), dma((n_seq,)),
            dma((4,)), dma((4,)),
            dma((2,)), dma((2,)),
            dma((2, 3)), dma((2, 3)),
            dma((2, 3)), dma((2, 3)),
            dma((3,)), dma((4,)),
        ],
        compiler_params=pltpu.CompilerParams(
            collective_id=0, has_side_effects=True, vmem_limit_bytes=56 * 1024 * 1024
        ),
        cost_estimate=pl.CostEstimate(
            flops=2 * rows * width * 4 * cols, bytes_accessed=2 * width * (4 * cols + 2 * half_width), transcendentals=0
        ),
        name="layer",
    )(
        patch_lengths, text_len, act[None, :],
        video.reshape(video_rows, width), text.reshape(text_rows, width), stale_cache.reshape(video_rows, 2, cols),
        w_mod[0], w_qkv[0].transpose(1, 0, 2), w_out[0],
    )
    hidden_video, hidden_text, cache_video, cache_text = pl.pallas_call(
        store_kernel,
        out_shape=tuple(jax.ShapeDtypeStruct(o.shape, o.dtype) for o in outputs),
        in_specs=[hbm] * 4,
        out_specs=(hbm,) * 4,
        scratch_shapes=[pltpu.VMEM(o.shape, o.dtype) for o in outputs] + [dma((2, 4))],
        compiler_params=pltpu.CompilerParams(vmem_limit_bytes=56 * 1024 * 1024),
        name="store",
    )(*outputs)
    return (
        hidden_video.reshape(1, requests, patches, per_dev, width),
        hidden_text.reshape(1, requests, text_dev, width),
        cache_video.reshape(1, requests, patches, per_dev, 2, cols),
        cache_text.reshape(1, requests, text_dev, 2, cols),
    )


def solution(mesh):
    placed = (
        P(None, None, "seq", None),
        P(None, "seq", None),
        P(),
        P(),
        P(),
        P("section", None, "mp"),
        P("section", None, None, "mp"),
        P("section", "mp", None),
        P("section", None, None, "seq", None, "mp"),
    )
    return jax.shard_map(
        body,
        mesh=mesh,
        in_specs=placed,
        out_specs=(
            P("section", None, None, "seq", None),
            P("section", None, "seq", None),
            P("section", None, None, "seq", None, "mp"),
            P("section", None, "seq", None, "mp"),
        ),
        check_vma=False,
    )
```

```python
import functools
import math

import jax
import jax.numpy as jnp
from jax import lax
from jax.experimental import pallas as pl
from jax.experimental.pallas import tpu as pltpu
from jax.sharding import PartitionSpec as P

HEAD = 64
EPS = 1e-05
NEG = -1e30
SLAB = 128
GROUP = 256
MESH = pl.DeviceIdType.MESH
F32 = jnp.float32
BF16 = jnp.bfloat16


def slot_marks(index, lengths_ref, text_ref, requests, first, patches, per_dev, text_dev, owner):
    req = jnp.zeros_like(index)
    patch = jnp.zeros_like(index)
    limit = jnp.zeros_like(index)
    start = jnp.zeros_like(index)
    at = 0
    for r in range(requests):
        for p in range(first, patches):
            inside = (index >= at) & (index < at + per_dev)
            req = jnp.where(inside, r, req)
            patch = jnp.where(inside, p, patch)
            limit = jnp.where(inside, lengths_ref[r, p], limit)
            start = jnp.where(inside, at, start)
            at += per_dev
    width = jnp.full_like(index, per_dev)
    for r in range(requests if text_dev else 0):
        inside = (index >= at) & (index < at + text_dev)
        req = jnp.where(inside, r, req)
        limit = jnp.where(inside, text_ref[r], limit)
        start = jnp.where(inside, at, start)
        width = jnp.where(inside, text_dev, width)
        at += text_dev
    live = owner * width + index - start < limit
    return req, patch, live


def split_index(shape, dim, size, count):
    index = lax.broadcasted_iota(jnp.int32, shape, dim)
    owner = jnp.zeros_like(index)
    for j in range(1, count):
        owner = owner + jnp.where(index >= j * size, 1, 0)
    return owner, index - owner * size


def kernel(dims, lengths_ref, text_len_ref, act_ref, video_ref, text_ref, stale_ref, w_mod_hbm,
           w_qkv_hbm, w_out_hbm, hidden_video, hidden_text, cache_video, cache_text,
           w_mod, w_qkv, w_out, x_buf, normed, projected, attended, result, mod_all, heads_send, heads_recv,
           back_send, back_recv, stale_held, cache_held, stale_send_buf, stale_recv_buf, key_cat, value_cat, part_send, part_recv, bias,
           w_sem, mod_send, mod_recv, stale_send, stale_recv, heads_out, heads_in, back_out, back_in, p_send, p_recv,
           cross_send, cross_recv, x_send, x_recv, res_send, res_recv, in_sem, out_sem):
    requests, patches, per_dev, text_dev, n_seq, n_mp, width, cols = dims
    rows = requests * (patches * per_dev + text_dev)
    video_rows = requests * patches * per_dev
    stale_rows = requests * (patches - 1) * per_dev
    groups = cols // GROUP
    each, active = head_split(cols // HEAD, n_seq)
    share = each * HEAD
    fresh_keys = n_seq * rows
    section = lax.axis_index("section")
    seq = lax.axis_index("seq")
    mp = lax.axis_index("mp")
    other = 1 - section
    core_mate = mp + 1 - 2 * lax.rem(mp, 2)
    y_mate = lax.rem(mp + 2, n_mp)
    diagonal = lax.rem(core_mate + 2, n_mp)
    half = rows // 32 * 16 + 16 * (rows // 16 % 2)
    row_pieces = (pl.ds(0, half), pl.ds(half, rows - half))
    row_slices = (slice(0, half), slice(half, rows))

    def at(sec, se, m):
        return (sec, se, m)

    mod_pieces = 4
    mod_piece = w_mod.shape[0] // mod_pieces
    mod_weights = [
        pltpu.make_async_copy(w_mod_hbm.at[pl.ds(i * mod_piece, mod_piece)], w_mod.at[pl.ds(i * mod_piece, mod_piece)],
                              w_sem.at[3 * groups + 1 + i]) for i in range(mod_pieces)]
    for copy in mod_weights:
        copy.start()
    in_copies = [
        pltpu.make_async_copy(video_ref, x_buf.at[pl.ds(0, video_rows)], in_sem.at[0]),
        pltpu.make_async_copy(text_ref, x_buf.at[pl.ds(video_rows, rows - video_rows)], in_sem.at[1]),
        pltpu.make_async_copy(stale_ref, stale_held, in_sem.at[2])]
    out_copies = [
        pltpu.make_async_copy(result.at[pl.ds(0, video_rows)], hidden_video, out_sem.at[0]),
        pltpu.make_async_copy(result.at[pl.ds(video_rows, rows - video_rows)], hidden_text, out_sem.at[1]),
        pltpu.make_async_copy(cache_held.at[pl.ds(0, video_rows)], cache_video, out_sem.at[2]),
        pltpu.make_async_copy(cache_held.at[pl.ds(video_rows, rows - video_rows)], cache_text, out_sem.at[3])]
    in_copies[2].start()

    @pl.when(section == 0)
    def _():
        in_copies[0].start()
        in_copies[1].start()

    weight_copies = []
    tile_order = sorted(range(groups), key=lambda g: min(g, groups - 1 - g))
    for g in tile_order:
        for part in range(3):
            weight_copies.append(pltpu.make_async_copy(
                w_qkv_hbm.at[part, :, pl.ds(g * GROUP, GROUP)],
                w_qkv.at[g, :, pl.ds(part * GROUP, GROUP)],
                w_sem.at[g * 3 + part]))
    weight_copies.append(pltpu.make_async_copy(w_out_hbm, w_out, w_sem.at[3 * groups]))
    barrier = pltpu.get_barrier_semaphore()
    for k in range(1, n_mp):
        pl.semaphore_signal(barrier, inc=1, device_id=at(section, seq, lax.rem(mp + k, n_mp)), device_id_type=MESH)
    for k in range(1, n_seq):
        pl.semaphore_signal(barrier, inc=1, device_id=at(section, lax.rem(seq + k, n_seq), mp), device_id_type=MESH)
    pl.semaphore_signal(barrier, inc=1, device_id=at(other, seq, mp), device_id_type=MESH)

    for copy in mod_weights:
        copy.wait()
    for copy in weight_copies:
        copy.start()
    act = jnp.broadcast_to(act_ref[...].astype(F32), (8, act_ref.shape[1])).astype(BF16)
    mod_all[mp] = jnp.dot(act, w_mod[...], preferred_element_type=F32)
    pl.semaphore_wait(barrier, n_mp - 1 + n_seq - 1 + 1)

    def mod_copy(k):
        return pltpu.make_async_remote_copy(
            src_ref=mod_all.at[mp], dst_ref=mod_all.at[mp], send_sem=mod_send.at[k],
            recv_sem=mod_recv.at[k], device_id=at(section, seq, lax.rem(mp + k, n_mp)), device_id_type=MESH)

    def mod_arrival(k):
        origin = lax.rem(mp + n_mp - k, n_mp)
        return pltpu.make_async_remote_copy(
            src_ref=mod_all.at[origin], dst_ref=mod_all.at[origin], send_sem=mod_send.at[k],
            recv_sem=mod_recv.at[k], device_id=at(section, seq, origin), device_id_type=MESH)

    def to_device(send, recv, sems, d):
        return pltpu.make_async_remote_copy(
            src_ref=send.at[d], dst_ref=recv.at[seq], send_sem=sems[0].at[d], recv_sem=sems[1].at[seq],
            device_id=at(section, d, mp), device_id_type=MESH)

    def from_device(send, recv, sems, origin):
        return pltpu.make_async_remote_copy(
            src_ref=recv.at[origin], dst_ref=recv.at[origin], send_sem=sems[0].at[origin], recv_sem=sems[1].at[origin],
            device_id=at(section, origin, mp), device_id_type=MESH)

    def send_part(exchange, d):
        @pl.when(seq != d)
        def _():
            to_device(*exchange, d).start()

    def keep_part(exchange, d):
        @pl.when(seq == d)
        def _():
            exchange[1][d] = exchange[0][d]

    def sent_part(exchange, d):
        @pl.when(seq != d)
        def _():
            to_device(*exchange, d).wait_send()

    stale_exchange = (stale_send_buf, stale_recv_buf, (stale_send, stale_recv))
    heads_exchange = (heads_send, heads_recv, (heads_out, heads_in))
    back_exchange = (back_send, back_recv, (back_out, back_in))

    def when_active(function):
        if active == n_seq:
            function()
        else:
            pl.when(seq < active)(function)

    for k in range(1, n_mp):
        mod_copy(k).start()

    span_all = patches * per_dev
    in_copies[2].wait()
    for kind in range(2):
        whole = stale_held[:, kind, :].astype(F32)
        kept = jnp.concatenate(
            [whole[r * span_all + per_dev:(r + 1) * span_all] for r in range(requests)], axis=0).astype(BF16)
        for d in range(active):
            stale_send_buf[d, :, kind * share:(kind + 1) * share] = kept[:, d * share:(d + 1) * share]
    for d in range(active):
        send_part(stale_exchange, d)
        keep_part(stale_exchange, d)

    row_index = lax.broadcasted_iota(jnp.int32, (rows, 1), 0)
    row_req, row_patch, _ = slot_marks(
        row_index, lengths_ref, text_len_ref, requests, 0, patches, per_dev, text_dev, 0)
    key_owner, key_index = split_index((1, n_seq * rows), 1, rows, n_seq)
    key_req, key_patch, key_live = slot_marks(
        key_index, lengths_ref, text_len_ref, requests, 0, patches, per_dev, text_dev, key_owner)
    key_limit = jnp.where(key_live, key_patch, patches)
    bias[:, :fresh_keys] = jnp.where((row_req == key_req) & (key_limit <= row_patch), 0.0, NEG)
    key_owner, key_index = split_index((1, n_seq * stale_rows), 1, stale_rows, n_seq)
    key_req, key_patch, key_live = slot_marks(
        key_index, lengths_ref, text_len_ref, requests, 1, patches, per_dev, 0, key_owner)
    key_limit = jnp.where(key_live, key_patch, -1)
    bias[:, fresh_keys:] = jnp.where((row_req == key_req) & (key_limit > row_patch), 0.0, NEG)

    @pl.when(section == 0)
    def _():
        in_copies[0].wait()
        in_copies[1].wait()

    def block(j):
        return pl.ds(pl.multiple_of(j * cols, SLAB), cols)

    def cross_copy(c):
        return pltpu.make_async_remote_copy(
            src_ref=result.at[row_pieces[c], block(mp)], dst_ref=x_buf.at[row_pieces[c], block(mp)],
            send_sem=cross_send.at[c], recv_sem=cross_recv.at[c], device_id=at(other, seq, mp), device_id_type=MESH)

    def spread_copy(buffer, sems, c, kind, origin):
        part = buffer.at[row_pieces[c], block(origin)]
        return pltpu.make_async_remote_copy(
            src_ref=part, dst_ref=part, send_sem=sems[0].at[c, kind], recv_sem=sems[1].at[c, kind],
            device_id=at(section, seq, y_mate if kind == 1 else core_mate), device_id_type=MESH)

    def spread_start(buffer, sems, c):
        spread_copy(buffer, sems, c, 1, mp).start()
        spread_copy(buffer, sems, c, 0, mp).start()

    def spread_finish(buffer, sems):
        for c in range(2):
            spread_copy(buffer, sems, c, 1, y_mate).wait_recv()
            spread_copy(buffer, sems, c, 2, y_mate).start()
        for c in range(2):
            spread_copy(buffer, sems, c, 0, core_mate).wait_recv()
            spread_copy(buffer, sems, c, 2, diagonal).wait_recv()

    def spread_sent(buffer, sems):
        for c in range(2):
            for kind, origin in enumerate((mp, mp, y_mate)):
                spread_copy(buffer, sems, c, kind, origin).wait_send()

    x_sems, result_sems = (x_send, x_recv), (res_send, res_recv)

    @pl.when(section == 1)
    def _():
        for c in range(2):
            cross_copy(c).wait_recv()
            spread_start(x_buf, x_sems, c)
        spread_finish(x_buf, x_sems)

    def modulated(b):
        return mod_all[b // 3, 0:1, (b % 3) * cols:(b % 3 + 1) * cols]

    values = x_buf[...].astype(F32)
    mean = jnp.mean(values, axis=-1, keepdims=True)
    center = values - mean
    inverse = lax.rsqrt(jnp.mean(center * center, axis=-1, keepdims=True) + EPS)
    for k in range(1, n_mp):
        mod_arrival(k).wait_recv()
    for c in range(n_mp):
        span = slice(c * cols, (c + 1) * cols)
        piece_values = (x_buf[:, span].astype(F32) - mean) * inverse
        normed[:, span] = (piece_values * (1.0 + modulated(n_mp + c)) + modulated(c)).astype(BF16)

    def project(g):
        return jnp.dot(normed[...], w_qkv[g], preferred_element_type=F32)

    middle = (n_seq + 1) // 2
    lower = 1 - seq // middle

    def project_all(order):
        done, sent = set(), set()
        for g in order:
            first_copy = 3 * tile_order.index(g)
            for copy in weight_copies[first_copy:first_copy + 3]:
                copy.wait()
            product = project(g)
            for part in range(3):
                tile = product[:, part * GROUP:(part + 1) * GROUP].astype(BF16)
                if part == 0:
                    tile = (tile.astype(F32) * HEAD ** (-0.5)).astype(BF16)
                projected[part, :, g * GROUP:(g + 1) * GROUP] = tile
            done.add(g)
            for d in sorted(range(active), reverse=order[0] != 0):
                first, last = d * share // GROUP, ((d + 1) * share - 1) // GROUP
                if d not in sent and all(t in done for t in range(first, last + 1)):
                    sent.add(d)
                    for part in range(3):
                        heads_send[d, :, part * share:(part + 1) * share] = (
                            projected[part, :, d * share:(d + 1) * share])
                    send_part(heads_exchange, d)
                    keep_part(heads_exchange, d)

    @pl.when(lower == 1)
    def _():
        project_all(tuple(reversed(range(groups))))

    @pl.when(lower == 0)
    def _():
        project_all(tuple(range(groups)))

    for g in range(groups):
        for kind in range(2):
            span = slice(g * GROUP, (g + 1) * GROUP)
            cache_held[:, kind, span] = projected[1 + kind, :, span]
    out_copies[2].start()
    out_copies[3].start()

    @when_active
    def _():
        for k in range(1, n_seq):
            from_device(*stale_exchange, lax.rem(seq + n_seq - k, n_seq)).wait_recv()
        for h in range(each):
            for kind, cat in enumerate((key_cat, value_cat)):
                at_col = kind * share + h * HEAD
                cat[h, fresh_keys:] = stale_recv_buf[:, :, at_col:at_col + HEAD].reshape(n_seq * stale_rows, HEAD)
        for k in range(1, n_seq):
            from_device(*heads_exchange, lax.rem(seq + n_seq - k, n_seq)).wait_recv()
        for h in range(each):
            for kind, cat in enumerate((key_cat, value_cat)):
                at_col = (1 + kind) * share + h * HEAD
                cat[h, :fresh_keys] = heads_recv[:, :, at_col:at_col + HEAD].reshape(fresh_keys, HEAD)
        for i in range(n_seq):
            d = i + lower * (n_seq - 1 - 2 * i)
            for h in range(each):
                heads_at = slice(h * HEAD, (h + 1) * HEAD)
                scores = lax.dot_general(
                    heads_recv[d, :, heads_at], key_cat[h], (((1,), (1,)), ((), ())), preferred_element_type=F32)
                scores = scores + bias[...]
                top = jnp.max(scores, axis=-1, keepdims=True)
                weights = jnp.exp(scores - top)
                total = jnp.sum(weights, axis=-1, keepdims=True)
                mixed = jnp.dot(weights.astype(BF16), value_cat[h], preferred_element_type=F32)
                back_send[d, :, heads_at] = (mixed / total).astype(BF16)
            send_part(back_exchange, d)
            keep_part(back_exchange, d)

    for d in range(active):
        @pl.when(seq != d)
        def _():
            from_device(*back_exchange, d).wait_recv()
    for d in range(active):
        attended[:, d * share:(d + 1) * share] = back_recv[d, :, :share]

    def part_copy(k):
        return pltpu.make_async_remote_copy(
            src_ref=part_send.at[k], dst_ref=part_recv.at[k], send_sem=p_send.at[k], recv_sem=p_recv.at[k],
            device_id=at(section, seq, core_mate), device_id_type=MESH)

    def y_copy(c):
        return pltpu.make_async_remote_copy(
            src_ref=part_send.at[2, row_pieces[c]], dst_ref=part_recv.at[2, row_pieces[c]],
            send_sem=p_send.at[2 + c], recv_sem=p_recv.at[2 + c],
            device_id=at(section, seq, y_mate), device_id_type=MESH)

    weight_copies[-1].wait()

    def out_block(j):
        return jnp.dot(attended[...], w_out[:, block(j)], preferred_element_type=F32)

    part_send[0] = out_block(diagonal).astype(BF16)
    part_copy(0).start()
    passed = out_block(y_mate)
    part_copy(0).wait_recv()
    for c in range(2):
        at_rows = row_slices[c]
        part_send[2, at_rows] = (passed[at_rows] + part_recv[0, at_rows].astype(F32)).astype(BF16)
        y_copy(c).start()
    part_send[1] = out_block(core_mate).astype(BF16)
    part_copy(1).start()
    summed = out_block(mp)
    part_copy(1).wait_recv()
    summed = summed + part_recv[1].astype(F32)
    gate_at = 2 * n_mp + mp
    gate = mod_all[gate_at // 3, 0:1, pl.ds(pl.multiple_of(gate_at % 3 * cols, SLAB), cols)]
    for c in range(2):
        at_rows = row_slices[c]
        y_copy(c).wait_recv()
        whole_sum = summed[at_rows] + part_recv[2, at_rows].astype(F32)
        result[at_rows, block(mp)] = (x_buf[at_rows, block(mp)].astype(F32) + gate * whole_sum).astype(BF16)

        @pl.when(section == 0)
        def _():
            cross_copy(c).start()

        spread_start(result, result_sems, c)
    spread_finish(result, result_sems)
    out_copies[0].start()
    out_copies[1].start()

    @pl.when(section == 0)
    def _():
        for c in range(2):
            cross_copy(c).wait_send()

    @pl.when(section == 1)
    def _():
        spread_sent(x_buf, x_sems)

    for copy in out_copies:
        copy.wait()
    spread_sent(result, result_sems)
    for k in range(1, n_mp):
        mod_copy(k).wait_send()
    for k in range(2):
        part_copy(k).wait_send()
        y_copy(k).wait_send()
    for d in range(active):
        sent_part(stale_exchange, d)
        sent_part(heads_exchange, d)

    @when_active
    def _():
        for d in range(n_seq):
            sent_part(back_exchange, d)


def store_kernel(*refs):
    ins, outs, held, sems = refs[:4], refs[4:8], refs[8:12], refs[12]
    loads = [pltpu.make_async_copy(ins[i], held[i], sems.at[0, i]) for i in range(4)]
    stores = [pltpu.make_async_copy(held[i], outs[i], sems.at[1, i]) for i in range(4)]
    for copy in loads:
        copy.start()
    for load, store in zip(loads, stores):
        load.wait()
        store.start()
    for copy in stores:
        copy.wait()


def padded(count):
    return -(-count // SLAB) * SLAB


def head_split(heads, n_seq):
    each = -(-heads // n_seq)
    while heads % each:
        each += 1
    return each, heads // each


def body(video, text, patch_lengths, text_len, timestep, w_mod, w_qkv, w_out, stale_cache):
    n_seq, n_mp = lax.axis_size("seq"), lax.axis_size("mp")
    requests, patches, per_dev, width = video.shape
    text_dev = text.shape[1]
    cols = w_out.shape[1]
    each, active = head_split(cols // HEAD, n_seq)
    share = each * HEAD
    rows = requests * (patches * per_dev + text_dev)
    video_rows = requests * patches * per_dev
    text_rows = requests * text_dev
    stale_rows = requests * (patches - 1) * per_dev

    half_width = w_mod.shape[1] // 2
    frequency = jnp.exp(-math.log(10000.0) * jnp.arange(half_width, dtype=F32) / half_width)
    phases = timestep.astype(F32)[0] * frequency
    embedding = jnp.concatenate([jnp.cos(phases), jnp.sin(phases)])
    act = jax.nn.silu(embedding).astype(BF16)

    mod_cols = w_mod.shape[2]
    keys = n_seq * (rows + stale_rows)
    dims = (requests, patches, per_dev, text_dev, n_seq, n_mp, width, cols)
    vmem = pl.BlockSpec(memory_space=pltpu.VMEM)
    smem = pl.BlockSpec(memory_space=pltpu.SMEM)
    hbm = pl.BlockSpec(memory_space=pl.ANY)
    dma = pltpu.SemaphoreType.DMA
    outputs = pl.pallas_call(
        functools.partial(kernel, dims),
        out_shape=(
            jax.ShapeDtypeStruct((video_rows, width), BF16),
            jax.ShapeDtypeStruct((text_rows, width), BF16),
            jax.ShapeDtypeStruct((video_rows, 2, cols), BF16),
            jax.ShapeDtypeStruct((text_rows, 2, cols), BF16),
        ),
        in_specs=[smem, smem, vmem] + [hbm] * 6,
        out_specs=(hbm,) * 4,
        scratch_shapes=[
            pltpu.VMEM(w_mod.shape[1:], BF16),
            pltpu.VMEM((cols // GROUP, width, 3 * GROUP), BF16),
            pltpu.VMEM((cols, width), BF16),
            pltpu.VMEM((rows, width), BF16),
            pltpu.VMEM((rows, width), BF16),
            pltpu.VMEM((3, rows, cols), BF16),
            pltpu.VMEM((rows, cols), BF16),
            pltpu.VMEM((rows, width), BF16),
            pltpu.VMEM((n_mp, 8, mod_cols), F32),
            pltpu.VMEM((active, rows, padded(3 * share)), BF16),
            pltpu.VMEM((n_seq, rows, padded(3 * share)), BF16),
            pltpu.VMEM((n_seq, rows, padded(share)), BF16),
            pltpu.VMEM((n_seq, rows, padded(share)), BF16),
            pltpu.VMEM((video_rows, 2, cols), BF16),
            pltpu.VMEM((rows, 2, cols), BF16),
            pltpu.VMEM((active, stale_rows, padded(2 * share)), BF16),
            pltpu.VMEM((n_seq, stale_rows, padded(2 * share)), BF16),
            pltpu.VMEM((each, keys, HEAD), BF16),
            pltpu.VMEM((each, keys, HEAD), BF16),
            pltpu.VMEM((3, rows, cols), BF16),
            pltpu.VMEM((3, rows, cols), BF16),
            pltpu.VMEM((rows, keys), F32),
            dma((3 * (cols // GROUP) + 5,)),
            dma((n_mp,)), dma((n_mp,)),
            dma((n_seq,)), dma((n_seq,)),
            dma((n_seq,)), dma((n_seq,)),
            dma((n_seq,)), dma((n_seq,)),
            dma((4,)), dma((4,)),
            dma((2,)), dma((2,)),
            dma((2, 3)), dma((2, 3)),
            dma((2, 3)), dma((2, 3)),
            dma((3,)), dma((4,)),
        ],
        compiler_params=pltpu.CompilerParams(
            collective_id=0, has_side_effects=True, vmem_limit_bytes=56 * 1024 * 1024
        ),
        cost_estimate=pl.CostEstimate(
            flops=2 * rows * width * 4 * cols, bytes_accessed=2 * width * (4 * cols + 2 * half_width), transcendentals=0
        ),
        name="layer",
    )(
        patch_lengths, text_len, act[None, :],
        video.reshape(video_rows, width), text.reshape(text_rows, width), stale_cache.reshape(video_rows, 2, cols),
        w_mod[0], w_qkv[0].transpose(1, 0, 2), w_out[0],
    )
    hidden_video, hidden_text, cache_video, cache_text = pl.pallas_call(
        store_kernel,
        out_shape=tuple(jax.ShapeDtypeStruct(o.shape, o.dtype) for o in outputs),
        in_specs=[hbm] * 4,
        out_specs=(hbm,) * 4,
        scratch_shapes=[pltpu.VMEM(o.shape, o.dtype) for o in outputs] + [dma((2, 4))],
        compiler_params=pltpu.CompilerParams(vmem_limit_bytes=56 * 1024 * 1024),
        name="store",
    )(*outputs)
    return (
        hidden_video.reshape(1, requests, patches, per_dev, width),
        hidden_text.reshape(1, requests, text_dev, width),
        cache_video.reshape(1, requests, patches, per_dev, 2, cols),
        cache_text.reshape(1, requests, text_dev, 2, cols),
    )


def solution(mesh):
    placed = (
        P(None, None, "seq", None),
        P(None, "seq", None),
        P(),
        P(),
        P(),
        P("section", None, "mp"),
        P("section", None, None, "mp"),
        P("section", "mp", None),
        P("section", None, None, "seq", None, "mp"),
    )
    return jax.shard_map(
        body,
        mesh=mesh,
        in_specs=placed,
        out_specs=(
            P("section", None, None, "seq", None),
            P("section", None, "seq", None),
            P("section", None, None, "seq", None, "mp"),
            P("section", None, "seq", None, "mp"),
        ),
        check_vma=False,
    )
```
